512 devices in a mesh: dp: 4 (over z_hi), node: 32 (over y, z_lo, core), chip: 4 (over x).
Axes of the slice: x: 4, y: 4, z: 16 (z_hi: 4, z_lo: 4; z = z_hi * 4 + z_lo), core: 2. Of those that a mesh axis runs over, the one named last changes fastest.
Arguments:
- se_gate: bfloat16 [65536, 2048], P(('dp', 'node', 'chip')), parts along dimension 0, may hold values from -6 to 6
- se_key: bfloat16 [65536, 2048], P(('dp', 'node', 'chip')), parts along dimension 0, may hold values from -6 to 6
- se_value: bfloat16 [65536, 2048], P(('dp', 'node', 'chip')), parts along dimension 0, may hold values from -6 to 6
- li_gate: bfloat16 [65536, 2048], P(('dp', 'node', 'chip')), parts along dimension 0, may hold values from -6 to 6
- li_key: bfloat16 [65536, 2048], P(('dp', 'node', 'chip')), parts along dimension 0, may hold values from -6 to 6
- li_value: bfloat16 [65536, 2048], P(('dp', 'node', 'chip')), parts along dimension 0, may hold values from -6 to 6
- se_feature: float32 [3, 3, 2048], replicated, may hold values from -3 to 3
- se_filter: float32 [7, 2048], replicated, may hold values from -2 to 2
- li_feature: float32 [3, 3, 2048], replicated, may hold values from -3 to 3
- li_residue: float32 [16, 2048], replicated, may hold values from -1.25 to 1.25
- li_rate: float32 [16, 2048], replicated, may hold values from 3.0517578e-06 to 0.08, as said below
- li_skip: float32 [2048], replicated, may hold values from -4 to 4
Outputs:
- se_out: bfloat16 [65536, 2048], P(('dp', 'node', 'chip')), parts along dimension 0
- li_out: bfloat16 [65536, 2048], P(('dp', 'node', 'chip')), parts along dimension 0
The draws below stay inside these ranges and needn't reach their ends.
There are 4 independent parts, one for each index of `dp`. The reference program is written for one: setup_inputs(seed, part) draws one part's arguments, and reference() takes and returns one part's arrays. A program takes and returns all parts, laid end to end along the dimension named above; an argument that names none is the same for every part. Nothing has to cross between parts.
Inputs may be any that keep to these rules, and one draw needn't show every extreme that they name: `li_rate`: positive decay rates.
All inputs are finite; a program needn't handle non-finite values.
Results may differ from the reference program's by a relative error of at most 0.0055.
Values may be sent and summed in bfloat16 or wider, within the bound.
No kernel may reach another device: no remote copies, remote signals or barrier semaphores. Data moves between devices by JAX's collectives and lax.ppermute only.
A program may use at most 64 MiB of HBM per device.

```python
import math
import jax
import jax.numpy as jnp
from jax import lax

CH = 2048
M = 16
SE_TAPS = 7
FEAT_TAPS = 3
LENGTH = 16384


def draw_li_rate(key, part):
    first, second, third = jax.random.split(jax.random.fold_in(key, 11), 3)
    slow = jnp.exp(jax.random.uniform(first, (M, CH), jnp.float32, math.log(0.05 / LENGTH), math.log(1.5 / LENGTH)))
    quick = jnp.exp(jax.random.uniform(second, (M, CH), jnp.float32, math.log(0.02), math.log(0.08)))
    share = 0.5
    picked = jax.random.uniform(third, (M, CH), jnp.float32) < share
    return jnp.where(picked, slow, quick).astype(jnp.float32)


def levels(key, dims, cuts, least, largest):
    def one(dim, parts):
        heights = jax.random.uniform(jax.random.fold_in(jax.random.fold_in(key, 6), dim), (parts,), jnp.float32, least / len(cuts), largest / len(cuts))
        return jnp.repeat(jnp.exp(heights), dims[dim] // parts).reshape((-1,) + (1,) * (len(dims) - dim - 1))

    gain = one(*cuts[0])
    for cut in cuts[1:]:
        gain = gain * one(*cut)
    return gain


def noise(key, shape, deviation, most, shards=(), held_as=jnp.bfloat16):
    entries = jax.random.normal(key, shape, jnp.float32) * deviation
    if len(shards) > 0:
        entries = levels(key, shape, shards, -0.22, 0.18) * entries
    return jnp.clip(entries, min=-most, max=most).astype(held_as)


def setup_inputs(seed: int = 0, part: int = 0) -> dict:
    arg_keys = jax.random.split(jax.random.key(seed), 13)
    part_splits = jax.random.split(jax.random.fold_in(arg_keys[12], part), 13)
    return {
        "se_gate": noise(part_splits[0], (LENGTH, CH), 1.0, 6.0, ((0, 128),)),
        "se_key": noise(part_splits[1], (LENGTH, CH), 1.0, 6.0, ((0, 128),)),
        "se_value": noise(part_splits[2], (LENGTH, CH), 1.0, 6.0, ((0, 128),)),
        "li_gate": noise(part_splits[3], (LENGTH, CH), 1.0, 6.0, ((0, 128),)),
        "li_key": noise(part_splits[4], (LENGTH, CH), 1.0, 6.0, ((0, 128),)),
        "li_value": noise(part_splits[5], (LENGTH, CH), 1.0, 6.0, ((0, 128),)),
        "se_feature": noise(arg_keys[6], (FEAT_TAPS, 3, CH), 0.6, 3.0, (), jnp.float32),
        "se_filter": noise(arg_keys[7], (SE_TAPS, CH), 0.4, 2.0, (), jnp.float32),
        "li_feature": noise(arg_keys[8], (FEAT_TAPS, 3, CH), 0.6, 3.0, (), jnp.float32),
        "li_residue": noise(arg_keys[9], (M, CH), 0.25, 1.25, (), jnp.float32),
        "li_rate": draw_li_rate(jax.random.fold_in(arg_keys[12], 71), part),
        "li_skip": noise(arg_keys[11], (CH,), 1.0, 4.0, (), jnp.float32),
    }


def delayed(field, lag):
    if lag == 0:
        return field
    empty = jnp.zeros((lag,) + field.shape[1:], field.dtype)
    return jnp.concatenate([empty, field[:-lag]], axis=0)

def causal_taps(field, taps):
    total = taps[0] * field
    for lag in range(1, taps.shape[0]):
        total = total + taps[lag] * delayed(field, lag)
    return total

def implicit_conv(values, residue, rate):
    length = values.shape[0]
    groups = values.shape[1] // 128
    modes = residue.shape[0]
    vblocks = values.reshape(length, groups, 128).transpose(1, 0, 2)
    rblocks = residue.reshape(modes, groups, 128).transpose(1, 0, 2)
    ablocks = rate.reshape(modes, groups, 128).transpose(1, 0, 2)

    def one_group(args):
        piece, resid, decay = args
        steps = jnp.arange(length, dtype=jnp.float32)
        weight = resid * jnp.sqrt(-jnp.expm1(-2.0 * decay))
        filt = lax.optimization_barrier(jnp.sum(weight[None] * jnp.exp(-steps[:, None, None] * decay[None]), axis=1))
        total = 2 * length
        spectrum = jnp.fft.rfft(piece, total, axis=0) * jnp.fft.rfft(filt, total, axis=0)
        return jnp.fft.irfft(spectrum, total, axis=0)[:length]
    result = lax.map(one_group, (vblocks, rblocks, ablocks))
    return result.transpose(1, 0, 2).reshape(length, groups * 128)

def reference(se_gate, se_key, se_value, li_gate, li_key, li_value, se_feature, se_filter, li_feature, li_residue, li_rate, li_skip):
    se_g = causal_taps(se_gate.astype(jnp.float32), se_feature[:, 0])
    se_k = causal_taps(se_key.astype(jnp.float32), se_feature[:, 1])
    se_v = causal_taps(se_value.astype(jnp.float32), se_feature[:, 2])
    u_se = (se_k * se_v).astype(jnp.bfloat16)
    mixed = causal_taps(u_se.astype(jnp.float32), se_filter)
    se_out = (se_g * mixed).astype(jnp.bfloat16)
    li_g = causal_taps(li_gate.astype(jnp.float32), li_feature[:, 0])
    li_k = causal_taps(li_key.astype(jnp.float32), li_feature[:, 1])
    li_v = causal_taps(li_value.astype(jnp.float32), li_feature[:, 2])
    u_li = (li_k * li_v).astype(jnp.bfloat16)
    flat = u_li.astype(jnp.float32)
    conv = implicit_conv(flat, li_residue, li_rate)
    li_out = (li_g * (conv + li_skip * flat)).astype(jnp.bfloat16)
    return (se_out, li_out)
```

```python
import functools

import jax
import jax.numpy as jnp
from jax import lax
from jax.experimental import pallas as pl
from jax.experimental.pallas import tpu as pltpu
from jax.sharding import Mesh, PartitionSpec as P

F32 = jnp.float32
BF16 = jnp.bfloat16
LANES = 128
NEAR = ("core", "chip")
FAR = "far"
PART = ("far", "core", "chip")
ROWS = 128
STEP = 16
GROUPS = ROWS // STEP
MODES = 16
VMEM_LIMIT = 16 * 1024 * 1024
HBM = pl.BlockSpec(memory_space=pltpu.HBM)
AUTO = None


SHORT_FLOPS = 50_000_000_000

def fast(*dims, dtype=F32):
    return pltpu.VMEM(dims, dtype)


def shape(*dims, dtype=F32):
    return jax.ShapeDtypeStruct(dims, dtype)


def slow(*dims, dtype=F32):
    return pltpu.HBM(dims, dtype)


def room(*dims, dtype=F32):
    return pltpu.VMEM(dims, dtype)


def call(kernel, name, ins, outs, scratch, flops, moved):
    whole = lambda spec: pl.BlockSpec(memory_space=pltpu.VMEM) if spec is None else spec
    many = len(outs) > 1
    inner = pl.pallas_call(
        kernel,
        out_shape=tuple(o for o, _ in outs) if many else outs[0][0],
        in_specs=[whole(spec) for spec in ins],
        out_specs=tuple(whole(spec) for _, spec in outs) if many else whole(outs[0][1]),
        name=name,
        scratch_shapes=list(scratch),
        compiler_params=pltpu.CompilerParams(vmem_limit_bytes=VMEM_LIMIT),
        cost_estimate=pl.CostEstimate(flops=flops, bytes_accessed=moved, transcendentals=0),
    )

    def outer(*values):
        return inner(
            *[pltpu.with_memory_space_constraint(v, pltpu.HBM) if spec is HBM else v for v, spec in zip(values, ins)]
        )

    return outer


def lanes_at(index):
    return pl.ds(pl.multiple_of(index * LANES, LANES), LANES)


def started(source, target, semaphore):
    copy = pltpu.make_async_copy(source, target, semaphore)
    copy.start()
    return copy


def pieces(width, count):
    size = width // count
    return [pl.ds(i * size, size) for i in range(count)]


def rim_kernel(seg, sek, sev, lig, lik, liv, after, out, tails, held, sems):
    del after
    copies = [started(ref.at[ROWS - 16 : ROWS], tails.at[i], sems.at[i]) for i, ref in enumerate((seg, sek, sev, lig, lik, liv))]
    held[24:32] = jnp.zeros_like(held[24:32])
    for copy in copies:
        copy.wait()
    held[0:8] = tails[1].astype(F32)[8:16]
    held[8:16] = tails[2].astype(F32)[8:16]
    held[16:18] = tails[0].astype(F32)[14:16]
    held[18:20] = tails[4].astype(F32)[14:16]
    held[20:22] = tails[5].astype(F32)[14:16]
    held[22:24] = tails[3].astype(F32)[14:16]
    out[...] = held[...].astype(BF16)


CHUNK = 8


def states_kernel(key_hbm, value_hbm, feature_hbm, rate_hbm, kept_hbm, sent_hbm, key, value, feature, rate, kept, sent, wide, fresh, sems, outs):
    width = key.shape[1]
    chunks = width // (CHUNK * LANES)
    spans = pieces(width, chunks)
    small = [started(feature_hbm, feature, sems.at[0]), started(rate_hbm, rate, sems.at[1])]
    large = [
        (
            started(key_hbm.at[:, span], key.at[:, span], sems.at[2 + 2 * i]),
            started(value_hbm.at[:, span], value.at[:, span], sems.at[3 + 2 * i]),
        )
        for i, span in enumerate(spans)
    ]
    for copy in small:
        copy.wait()

    def featurized(ref, stream, lanes, slot):
        raw = ref[:, lanes].astype(F32)
        wide[slot, stream, 8 : 8 + ROWS] = raw
        return (
            feature[0, stream : stream + 1, lanes] * raw
            + feature[1, stream : stream + 1, lanes] * wide[slot, stream, 7 : 7 + ROWS]
            + feature[2, stream : stream + 1, lanes] * wide[slot, stream, 6 : 6 + ROWS]
        )

    wide[:, :, 0:8] = jnp.zeros((2, 3, 8, LANES), F32)
    leaving = []
    for index in range(chunks):
        for copy in large[index]:
            copy.wait()
        decays = []
        for part in range(CHUNK):
            block = index * CHUNK + part
            lanes = pl.ds(block * LANES, LANES)
            owner = block // 2
            half = slice((part % 2) * LANES, (part % 2 + 1) * LANES)
            slot = part % 2
            u = featurized(key, 1, lanes, slot) * featurized(value, 2, lanes, slot)
            fresh[part] = u.astype(BF16).astype(F32)
            fresh[part, 0:2] = jnp.zeros((2, LANES), F32)
            sent[owner, 16:18, half] = wide[slot, 1, 8:10]
            sent[owner, 18:20, half] = wide[slot, 2, 8:10]
            sent[owner, 20:22, half] = wide[slot, 1, ROWS + 6 : ROWS + 8]
            sent[owner, 22:24, half] = wide[slot, 2, ROWS + 6 : ROWS + 8]
            decays.append(jnp.exp(-rate[:, lanes]))

        def group(g, states):
            for part in range(CHUNK):
                kept[g, :, pl.ds((index * CHUNK + part) * LANES, LANES)] = states[part]
            states = list(states)
            for t in range(STEP):
                for part in range(CHUNK):
                    row = fresh[part, pl.ds(g * STEP + t, 1), :]
                    states[part] = decays[part] * states[part] + row
            return tuple(states)

        zero = jnp.zeros((MODES, LANES), F32)
        states = lax.fori_loop(0, GROUPS, group, (zero,) * CHUNK)
        for part in range(CHUNK):
            half = slice((part % 2) * LANES, (part % 2 + 1) * LANES)
            sent[(index * CHUNK + part) // 2, 0:MODES, half] = states[part]
        owners = pl.ds(index * CHUNK // 2, CHUNK // 2)
        leaving.append(started(sent.at[owners], sent_hbm.at[owners], outs.at[2 * index]))
        leaving.append(started(kept.at[:, :, spans[index]], kept_hbm.at[:, :, spans[index]], outs.at[2 * index + 1]))
    for copy in leaving:
        copy.wait()


def first_two(taps, own, before):
    def pair(base, tap):
        zero, one = own[base : base + 1], own[base + 1 : base + 2]
        two_ago, one_ago = before[base : base + 1], before[base + 1 : base + 2]
        return (
            tap[0] * zero + tap[1] * one_ago + tap[2] * two_ago,
            tap[0] * one + tap[1] * zero + tap[2] * one_ago,
        )

    k0, k1 = pair(0, taps[0])
    v0, v1 = pair(2, taps[1])
    return ((k0 * v0).astype(BF16).astype(F32), (k1 * v1).astype(BF16).astype(F32))


def owned(feature, rate, chips):
    width = 2 * LANES
    me = lax.axis_index("core") * chips + lax.axis_index("chip")
    lanes = pl.ds(pl.multiple_of(me * width, width), width)
    taps = [[feature[j, s : s + 1, lanes] for j in range(3)] for s in (1, 2)]
    return taps, rate[:, lanes]


def group_kernel(chips, came, feature, rate, sent_hbm, full_hbm, sent, full, sems):
    taps, pace = owned(feature, rate, chips)
    e_block = jnp.exp(-float(ROWS) * pace)
    e_first = jnp.exp(-float(ROWS - 1) * pace)
    e_second = jnp.exp(-float(ROWS - 2) * pace)
    peers = came.shape[0]
    total = came[0, 0:MODES]
    full[0] = total
    for i in range(1, peers):
        u0, u1 = first_two(taps, came[i, 16:20], came[i - 1, 20:24])
        mine = came[i, 0:MODES] + e_first * u0 + e_second * u1
        full[i] = mine
        total = e_block * total + mine
    rims = jnp.concatenate([came[0, 16:20], came[peers - 1, 20:24]], axis=0)
    sent[...] = jnp.concatenate([total, rims], axis=0).astype(BF16)
    copies = [started(sent, sent_hbm.at[i], sems.at[i]) for i in range(sent_hbm.shape[0])]
    copies.append(started(full, full_hbm, sems.at[sent_hbm.shape[0]]))
    for copy in copies:
        copy.wait()


def carry_kernel(chips, came, full_hbm, feature, rate, out_hbm, full, out, sems):
    arriving = started(full_hbm, full, sems.at[0])
    taps, pace = owned(feature, rate, chips)
    me = lax.axis_index(FAR)
    peers = full.shape[0]
    span = float(ROWS * peers)
    e_group = jnp.exp(-span * pace)
    g_first = jnp.exp(-(span - 1.0) * pace)
    g_second = jnp.exp(-(span - 2.0) * pace)
    e_block = jnp.exp(-float(ROWS) * pace)
    e_first = jnp.exp(-float(ROWS - 1) * pace)
    e_second = jnp.exp(-float(ROWS - 2) * pace)
    carry = jnp.zeros_like(pace)
    before = jnp.zeros((4, pace.shape[1]), F32)
    own0 = jnp.zeros((1, pace.shape[1]), F32)
    own1 = own0
    for i in range(came.shape[0]):
        block = came[i].astype(F32)
        u0, u1 = first_two(taps, block[16:20], before)
        before = block[20:24]
        total = block[0:MODES] + g_first * u0 + g_second * u1
        carry = jnp.where(i < me, e_group * carry + total, carry)
        own0 = jnp.where(i == me, u0, own0)
        own1 = jnp.where(i == me, u1, own1)
    arriving.wait()
    out[0] = carry
    carry = e_block * carry + (full[0] + e_first * own0 + e_second * own1)
    for i in range(1, peers):
        out[i] = carry
        carry = e_block * carry + full[i]
    started(out, out_hbm, sems.at[1]).wait()


def reach_kernel(rate, weight, out):
    place = (lax.broadcasted_iota(jnp.int32, (STEP, LANES), 0) + 1).astype(F32)

    def block(index, carry):
        lanes = lanes_at(index)
        total = jnp.zeros((STEP, LANES), F32)
        for m in range(MODES):
            tap = weight[m : m + 1, lanes] * jnp.exp(-place * rate[m : m + 1, lanes])
            out[m, :, lanes] = tap
            total = total + tap
        out[MODES, :, lanes] = total
        now = jnp.sum(weight[:, lanes], axis=0, keepdims=True)
        out[MODES, STEP - 1 : STEP, lanes] = now
        return carry

    lax.fori_loop(0, rate.shape[1] // LANES, block, 0)


SHORT_PIECES = 4


def short_kernel(
    gate_hbm, key_hbm, value_hbm, rim_hbm, feature_hbm, taps_hbm, out_hbm, gate, key, value, rim, feature, taps, out, kw, vw, gw, uw, sems, outs
):
    width = key.shape[1]
    spans = pieces(width, SHORT_PIECES)
    small = [
        started(rim_hbm, rim, sems.at[0]),
        started(feature_hbm, feature, sems.at[1]),
        started(taps_hbm, taps, sems.at[2]),
    ]
    large = [
        [started(a.at[:, span], b.at[:, span], sems.at[3 + 3 * i + j]) for j, (a, b) in enumerate(((gate_hbm, gate), (key_hbm, key), (value_hbm, value)))]
        for i, span in enumerate(spans)
    ]
    for slot in range(2):
        kw[slot, 0:8] = jnp.zeros((8, LANES), F32)
        vw[slot, 0:8] = jnp.zeros((8, LANES), F32)
        gw[slot, 0:16] = jnp.zeros((16, LANES), F32)
    for copy in small:
        copy.wait()

    def one(block, slot):
        lanes = lanes_at(block)
        halo = rim[:, lanes].astype(F32)
        kw[slot, 8:16] = halo[0:8]
        kw[slot, 16 : 16 + ROWS] = key[:, lanes].astype(F32)
        vw[slot, 8:16] = halo[8:16]
        vw[slot, 16 : 16 + ROWS] = value[:, lanes].astype(F32)
        gw[slot, 14:16] = halo[16:18]
        gw[slot, 16 : 16 + ROWS] = gate[:, lanes].astype(F32)

        def feat(w, stream, start, count):
            f = [feature[j, stream : stream + 1, lanes] for j in range(3)]
            return (
                f[0] * w[slot, start : start + count]
                + f[1] * w[slot, start - 1 : start - 1 + count]
                + f[2] * w[slot, start - 2 : start - 2 + count]
            )

        u = feat(kw, 1, 8, ROWS + 8) * feat(vw, 2, 8, ROWS + 8)
        uw[slot] = u.astype(BF16).astype(F32)
        mixed = taps[0:1, lanes] * uw[slot, 8 : 8 + ROWS]
        for lag in range(1, taps.shape[0]):
            mixed = mixed + taps[lag : lag + 1, lanes] * uw[slot, 8 - lag : 8 - lag + ROWS]
        out[:, lanes] = (feat(gw, 0, 16, ROWS) * mixed).astype(BF16)

    each = width // SHORT_PIECES // LANES // 2
    leaving = []
    for i, span in enumerate(spans):
        for copy in large[i]:
            copy.wait()

        def pair(index, carry):
            for slot in range(2):
                one((i * each + index) * 2 + slot, slot)
            return carry

        lax.fori_loop(0, each, pair, 0)
        leaving.append(started(out.at[:, span], out_hbm.at[:, span], outs.at[i]))
    for copy in leaving:
        copy.wait()


LOCAL_PIECES = 4


def local_kernel(
    gate_hbm, key_hbm, value_hbm, rim_hbm, feature_hbm, skip_hbm, kept_hbm, reach, rate, out_hbm, out, gate, key, value, rim, feature, skip, kept, kw, vw, gw, uw, sems, outs
):
    width = key.shape[1]
    spans = pieces(width, LOCAL_PIECES)
    small = [
        started(rim_hbm, rim, sems.at[0]),
        started(feature_hbm, feature, sems.at[1]),
        started(skip_hbm, skip, sems.at[2]),
    ]
    large = [
        [
            started(a.at[:, span], b.at[:, span], sems.at[3 + 4 * i + j])
            for j, (a, b) in enumerate(((gate_hbm, gate), (key_hbm, key), (value_hbm, value)))
        ]
        + [started(kept_hbm.at[:, :, span], kept.at[:, :, span], sems.at[6 + 4 * i])]
        for i, span in enumerate(spans)
    ]
    for w in (kw, vw, gw, uw):
        for slot in range(2):
            w[slot, 0:16] = jnp.zeros((16, LANES), F32)
    place = lax.broadcasted_iota(jnp.int32, (STEP, LANES), 0)
    for copy in small:
        copy.wait()

    def one(block, slot):
        lanes = lanes_at(block)
        halo = rim[:, lanes].astype(F32)
        kw[slot, 14:16] = halo[18:20]
        kw[slot, 16 : 16 + ROWS] = key[:, lanes].astype(F32)
        vw[slot, 14:16] = halo[20:22]
        vw[slot, 16 : 16 + ROWS] = value[:, lanes].astype(F32)
        gw[slot, 14:16] = halo[22:24]
        gw[slot, 16 : 16 + ROWS] = gate[:, lanes].astype(F32)

        def feat(w, stream):
            f = [feature[j, stream : stream + 1, lanes] for j in range(3)]
            return f[0] * w[slot, 16 : 16 + ROWS] + f[1] * w[slot, 15 : 15 + ROWS] + f[2] * w[slot, 14 : 14 + ROWS]

        out[ROWS : 2 * ROWS, lanes] = feat(gw, 0)
        uw[slot, 16 : 16 + ROWS] = (feat(kw, 1) * feat(vw, 2)).astype(BF16).astype(F32)
        pace = rate[:, lanes]
        jump = jnp.exp(-float(STEP) * pace)
        state = uw[slot, 16:17] * jnp.exp(-float(STEP - 1) * pace) + uw[slot, 17:18] * jnp.exp(-float(STEP - 2) * pace)
        for g in range(1, GROUPS):
            out[2 * ROWS + g * MODES : 2 * ROWS + (g + 1) * MODES, lanes] = kept[g, :, lanes] + state
            state = state * jump
        now = reach[MODES, STEP - 1 : STEP, lanes] + skip[:, lanes]
        low, high = [], []
        for g in range(GROUPS):
            start = 16 + g * STEP
            low.append(now * uw[slot, start : start + 8])
            high.append(now * uw[slot, start + 8 : start + STEP])
        for lag in range(1, STEP):
            tap = jnp.where(place >= lag, reach[MODES, lag - 1 : lag, lanes], 0.0)
            for g in range(GROUPS):
                start = 16 + g * STEP - lag
                if lag < 8:
                    low[g] = low[g] + tap[0:8] * uw[slot, start : start + 8]
                high[g] = high[g] + tap[8:STEP] * uw[slot, start + 8 : start + STEP]
        for g in range(GROUPS):
            out[g * STEP : g * STEP + 8, lanes] = low[g]
            out[g * STEP + 8 : (g + 1) * STEP, lanes] = high[g]

    each = width // LOCAL_PIECES // LANES // 2
    leaving = []
    for i, span in enumerate(spans):
        for copy in large[i]:
            copy.wait()

        def pair(index, carry):
            for slot in range(2):
                one((i * each + index) * 2 + slot, slot)
            return carry

        lax.fori_loop(0, each, pair, 0)
        leaving.append(started(out.at[:, span], out_hbm.at[:, span], outs.at[i]))
    for copy in leaving:
        copy.wait()


FINISH_PIECES = 4


def finish_kernel(came, local_hbm, reach, rate, out_hbm, local, out, rows, sems, outs):
    width = rate.shape[1]
    spans = pieces(width, FINISH_PIECES)
    arriving = [started(local_hbm.at[:, span], local.at[:, span], sems.at[i]) for i, span in enumerate(spans)]
    each = width // FINISH_PIECES // LANES // 2

    def one(owner, slot):
        lanes = lanes_at(owner * 2 + slot)
        state = came[owner, :, slot * LANES : (slot + 1) * LANES]
        rows[slot, 0:MODES] = state
        jump = jnp.exp(-float(STEP) * rate[:, lanes])
        for g in range(1, GROUPS):
            state = state * jump
            rows[slot, g * MODES : (g + 1) * MODES] = state + local[2 * ROWS + g * MODES : 2 * ROWS + (g + 1) * MODES, lanes]
        totals = [local[g * STEP : (g + 1) * STEP, lanes] for g in range(GROUPS)]
        for m in range(MODES):
            tap = reach[m, :, lanes]
            for g in range(GROUPS):
                totals[g] = totals[g] + tap * rows[slot, g * MODES + m : g * MODES + m + 1]
        for g in range(GROUPS):
            total = local[ROWS + g * STEP : ROWS + (g + 1) * STEP, lanes] * totals[g]
            out[g * STEP : (g + 1) * STEP, lanes] = total.astype(BF16)

    leaving = []
    for i, span in enumerate(spans):

        def pair(index, carry):
            for slot in range(2):
                one(i * each + index, slot)
            return carry

        arriving[i].wait()
        lax.fori_loop(0, each, pair, 0)
        leaving.append(started(out.at[:, span], out_hbm.at[:, span], outs.at[i]))
    for copy in leaving:
        copy.wait()


def shards(
    se_gate,
    se_key,
    se_value,
    li_gate,
    li_key,
    li_value,
    se_feature,
    se_filter,
    li_feature,
    li_residue,
    li_rate,
    li_skip,
):
    width = se_gate.shape[1]
    chips = lax.axis_size("chip")
    near = lax.axis_size(NEAR)
    far = lax.axis_size(FAR)
    part = width // near
    swap = lambda value, axis: lax.all_to_all(value, axis, split_axis=0, concat_axis=0, tiled=True)
    dma = pltpu.SemaphoreType.DMA
    stream = room(ROWS, width, dtype=BF16)
    padded = room(2, 16 + ROWS, LANES)
    rim_room = room(32, width, dtype=BF16)
    feature_room = room(*li_feature.shape)

    kept, sent = call(
        states_kernel,
        "states",
        [HBM] * 4,
        [(slow(GROUPS, MODES, width), HBM), (slow(near, 24, part), HBM)],
        [
            stream,
            stream,
            feature_room,
            room(MODES, width),
            room(GROUPS, MODES, width),
            room(near, 24, part),
            room(2, 3, 8 + ROWS, LANES),
            room(CHUNK, ROWS, LANES),
            dma((2 + 2 * (width // (CHUNK * LANES)),)),
            dma((2 * (width // (CHUNK * LANES)),)),
        ],
        12000000,
        3000000,
    )(li_key, li_value, li_feature, li_rate)

    came = swap(sent, NEAR)
    rim = call(
        rim_kernel,
        "rim",
        [HBM] * 7,
        [(fast(32, width, dtype=BF16), AUTO)],
        [room(6, 16, width, dtype=BF16), room(32, width), dma((6,))],
        1000000,
        500000,
    )(se_gate, se_key, se_value, li_gate, li_key, li_value, kept)
    weight = li_residue * jnp.sqrt(-jnp.expm1(-2.0 * li_rate))
    reach = call(
        reach_kernel, "reach", [AUTO] * 2, [(fast(MODES + 1, STEP, width), AUTO)], [], 3000000, 2000000
    )(li_rate, weight)
    came, reach = lax.optimization_barrier((came, reach))

    group, full = call(
        functools.partial(group_kernel, chips),
        "group",
        [AUTO] * 3,
        [(slow(far, 24, part, dtype=BF16), HBM), (slow(near, MODES, part), HBM)],
        [room(24, part, dtype=BF16), room(near, MODES, part), dma((far + 1,))],
        500000,
        500000,
    )(came, li_feature, li_rate)

    groups = swap(group, FAR)
    count = lax.axis_size(PART)
    halo = lax.ppermute(rim, PART, [(i, i + 1) for i in range(count - 1)])
    se_out = call(
        short_kernel,
        "short",
        [HBM] * 6,
        [(slow(ROWS, width, dtype=BF16), HBM)],
        [
            stream,
            stream,
            stream,
            rim_room,
            feature_room,
            room(*se_filter.shape),
            stream,
            padded,
            padded,
            padded,
            room(2, 8 + ROWS, LANES),
            dma((3 + 3 * SHORT_PIECES,)),
            dma((SHORT_PIECES,)),
        ],
        SHORT_FLOPS,
        2000000,
    )(se_gate, se_key, se_value, halo, se_feature, se_filter)
    groups, se_out = lax.optimization_barrier((groups, se_out))

    states = call(
        functools.partial(carry_kernel, chips),
        "carry",
        [AUTO, HBM, AUTO, AUTO],
        [(slow(near, MODES, part), HBM)],
        [room(near, MODES, part), room(near, MODES, part), dma((2,))],
        500000,
        500000,
    )(groups, full, li_feature, li_rate)

    back = swap(states, NEAR)
    local = call(
        local_kernel,
        "local",
        [HBM] * 7 + [AUTO] * 2,
        [(slow(3 * ROWS, width), HBM)],
        [
            room(3 * ROWS, width),
            stream,
            stream,
            stream,
            rim_room,
            feature_room,
            room(1, width),
            room(GROUPS, MODES, width),
            padded,
            padded,
            padded,
            padded,
            dma((3 + 4 * LOCAL_PIECES,)),
            dma((LOCAL_PIECES,)),
        ],
        12000000,
        3000000,
    )(li_gate, li_key, li_value, halo, li_feature, li_skip.reshape(1, width), kept, reach, li_rate)

    li_out = call(
        finish_kernel,
        "finish",
        [AUTO, HBM, AUTO, AUTO],
        [(slow(ROWS, width, dtype=BF16), HBM)],
        [room(3 * ROWS, width), stream, room(2, GROUPS * MODES, LANES), dma((FINISH_PIECES,)), dma((FINISH_PIECES,))],
        10000000,
        5000000,
    )(back, local, reach, li_rate)
    return (se_out, li_out)


def solution(mesh):
    sizes = dict(zip(mesh.axis_names, mesh.devices.shape))
    split = mesh.devices.reshape(sizes["dp"], sizes["node"] // 2, 2, sizes["chip"])
    inner = Mesh(split, ("dp", "far", "core", "chip"))
    rows = P(("dp", "far", "core", "chip"), None)
    return jax.shard_map(
        shards,
        mesh=inner,
        in_specs=(rows,) * 6 + (P(),) * 6,
        out_specs=(rows, rows),
        check_vma=False,
    )
```

```python
import functools

import jax
import jax.numpy as jnp
from jax import lax
from jax.experimental import pallas as pl
from jax.experimental.pallas import tpu as pltpu
from jax.sharding import Mesh, PartitionSpec as P

F32 = jnp.float32
BF16 = jnp.bfloat16
LANES = 128
NEAR = ("core", "chip")
FAR = "far"
PART = ("far", "core", "chip")
ROWS = 128
STEP = 16
GROUPS = ROWS // STEP
HALF = STEP // 2
MODES = 16
VMEM_LIMIT = 16 * 1024 * 1024
HBM = pl.BlockSpec(memory_space=pltpu.HBM)
AUTO = None


LOCAL_FLOPS = 50_000_000_000

def fast(*dims, dtype=F32):
    return pltpu.VMEM(dims, dtype)


def shape(*dims, dtype=F32):
    return jax.ShapeDtypeStruct(dims, dtype)


def slow(*dims, dtype=F32):
    return pltpu.HBM(dims, dtype)


def room(*dims, dtype=F32):
    return pltpu.VMEM(dims, dtype)


def call(kernel, name, ins, outs, scratch, flops, moved):
    whole = lambda spec: pl.BlockSpec(memory_space=pltpu.VMEM) if spec is None else spec
    many = len(outs) > 1
    inner = pl.pallas_call(
        kernel,
        out_shape=tuple(o for o, _ in outs) if many else outs[0][0],
        in_specs=[whole(spec) for spec in ins],
        out_specs=tuple(whole(spec) for _, spec in outs) if many else whole(outs[0][1]),
        name=name,
        scratch_shapes=list(scratch),
        compiler_params=pltpu.CompilerParams(vmem_limit_bytes=VMEM_LIMIT),
        cost_estimate=pl.CostEstimate(flops=flops, bytes_accessed=moved, transcendentals=0),
    )

    def outer(*values):
        return inner(
            *[pltpu.with_memory_space_constraint(v, pltpu.HBM) if spec is HBM else v for v, spec in zip(values, ins)]
        )

    return outer


def lanes_at(index):
    return pl.ds(pl.multiple_of(index * LANES, LANES), LANES)


def started(source, target, semaphore):
    copy = pltpu.make_async_copy(source, target, semaphore)
    copy.start()
    return copy


def piece(width, count, index):
    size = width // count
    return pl.ds(pl.multiple_of(index * size, size), size)


def over(count, body):
    lax.fori_loop(0, count, lambda index, carry: body(index) or carry, 0)


def rim_kernel(seg, sek, sev, lig, lik, liv, after, out, tails, held, sems):
    del after
    copies = [started(ref.at[ROWS - 16 : ROWS], tails.at[i], sems.at[i]) for i, ref in enumerate((seg, sek, sev, lig, lik, liv))]
    held[24:32] = jnp.zeros_like(held[24:32])
    for copy in copies:
        copy.wait()
    held[0:8] = tails[1].astype(F32)[8:16]
    held[8:16] = tails[2].astype(F32)[8:16]
    held[16:18] = tails[0].astype(F32)[14:16]
    held[18:20] = tails[4].astype(F32)[14:16]
    held[20:22] = tails[5].astype(F32)[14:16]
    held[22:24] = tails[3].astype(F32)[14:16]
    out[...] = held[...].astype(BF16)


CHUNK = 4


def states_kernel(key_hbm, value_hbm, feature_hbm, rate_hbm, kept_hbm, sent_hbm, key, value, feature, rate, kept, sent, wide, fresh, sems, outs):
    width = key.shape[1]
    chunks = width // (CHUNK * LANES)

    def large(index):
        span = piece(width, chunks, index)
        return [
            pltpu.make_async_copy(key_hbm.at[:, span], key.at[:, span], sems.at[2 + 2 * index]),
            pltpu.make_async_copy(value_hbm.at[:, span], value.at[:, span], sems.at[3 + 2 * index]),
        ]

    def leaving(index):
        span = piece(width, chunks, index)
        owners = pl.ds(index * (CHUNK // 2), CHUNK // 2)
        return [
            pltpu.make_async_copy(sent.at[owners], sent_hbm.at[owners], outs.at[2 * index]),
            pltpu.make_async_copy(kept.at[:, :, span], kept_hbm.at[:, :, span], outs.at[2 * index + 1]),
        ]

    small = [started(feature_hbm, feature, sems.at[0]), started(rate_hbm, rate, sems.at[1])]
    for index in range(chunks):
        for copy in large(index):
            copy.start()
    for copy in small:
        copy.wait()

    def featurized(ref, stream, lanes, slot):
        raw = ref[:, lanes].astype(F32)
        wide[slot, stream, 8 : 8 + ROWS] = raw
        return (
            feature[0, stream : stream + 1, lanes] * raw
            + feature[1, stream : stream + 1, lanes] * wide[slot, stream, 7 : 7 + ROWS]
            + feature[2, stream : stream + 1, lanes] * wide[slot, stream, 6 : 6 + ROWS]
        )

    wide[:, :, 0:8] = jnp.zeros((2, 3, 8, LANES), F32)

    def chunk(index):
        for copy in large(index):
            copy.wait()
        decays = []
        for part in range(CHUNK):
            block = index * CHUNK + part
            lanes = lanes_at(block)
            owner = index * (CHUNK // 2) + part // 2
            half = slice((part % 2) * LANES, (part % 2 + 1) * LANES)
            slot = part % 2
            u = featurized(key, 1, lanes, slot) * featurized(value, 2, lanes, slot)
            fresh[part] = u.astype(BF16).astype(F32)
            fresh[part, 0:2] = jnp.zeros((2, LANES), F32)
            sent[owner, 16:18, half] = wide[slot, 1, 8:10]
            sent[owner, 18:20, half] = wide[slot, 2, 8:10]
            sent[owner, 20:22, half] = wide[slot, 1, ROWS + 6 : ROWS + 8]
            sent[owner, 22:24, half] = wide[slot, 2, ROWS + 6 : ROWS + 8]
            decays.append([jnp.exp(-times * rate[:, lanes]) for times in (1.0, 2.0, 4.0)])
        states = [jnp.zeros((MODES, LANES), F32)] * CHUNK
        for t in range(0, ROWS, 4):
            for part in range(CHUNK):
                if t % STEP == 0:
                    kept[t // STEP, :, lanes_at(index * CHUNK + part)] = states[part]
                row = [fresh[part, t + i : t + i + 1, :] for i in range(4)]
                one, two, four = decays[part]
                first = one * row[0] + row[1]
                second = one * row[2] + row[3]
                states[part] = four * states[part] + (two * first + second)
        for part in range(CHUNK):
            half = slice((part % 2) * LANES, (part % 2 + 1) * LANES)
            sent[index * (CHUNK // 2) + part // 2, 0:MODES, half] = states[part]
        for copy in leaving(index):
            copy.start()

    over(chunks, chunk)
    for index in range(chunks):
        for copy in leaving(index):
            copy.wait()


def first_two(taps, own, before):
    def pair(base, tap):
        zero, one = own[base : base + 1], own[base + 1 : base + 2]
        two_ago, one_ago = before[base : base + 1], before[base + 1 : base + 2]
        return (
            tap[0] * zero + tap[1] * one_ago + tap[2] * two_ago,
            tap[0] * one + tap[1] * zero + tap[2] * one_ago,
        )

    k0, k1 = pair(0, taps[0])
    v0, v1 = pair(2, taps[1])
    return ((k0 * v0).astype(BF16).astype(F32), (k1 * v1).astype(BF16).astype(F32))


def owned_lanes(chips, width):
    me = lax.axis_index("core") * chips + lax.axis_index("chip")
    return pl.ds(pl.multiple_of(me * width, width), width)


def taps_of(feature):
    return [[feature[j, s : s + 1] for j in range(3)] for s in (1, 2)]


def group_kernel(chips, came, feature, rate, sent_hbm, full_hbm, sent, full, sems):
    lanes = owned_lanes(chips, came.shape[2])
    taps = [[feature[j, s : s + 1, lanes] for j in range(3)] for s in (1, 2)]
    pace = rate[:, lanes]
    e_block = jnp.exp(-float(ROWS) * pace)
    e_first = jnp.exp(-float(ROWS - 1) * pace)
    e_second = jnp.exp(-float(ROWS - 2) * pace)
    peers = came.shape[0]
    total = came[0, 0:MODES]
    full[0] = total
    for i in range(1, peers):
        u0, u1 = first_two(taps, came[i, 16:20], came[i - 1, 20:24])
        mine = came[i, 0:MODES] + e_first * u0 + e_second * u1
        full[i] = mine
        total = e_block * total + mine
    rims = jnp.concatenate([came[0, 16:20], came[peers - 1, 20:24]], axis=0)
    sent[...] = jnp.concatenate([total, rims], axis=0).astype(BF16)
    copies = [started(sent, sent_hbm.at[i], sems.at[i]) for i in range(sent_hbm.shape[0])]
    copies.append(started(full, full_hbm, sems.at[sent_hbm.shape[0]]))
    for copy in copies:
        copy.wait()


def carry_kernel(chips, came, full_hbm, feature_hbm, rate, out_hbm, full, out, feature, sems):
    lanes = owned_lanes(chips, came.shape[2])
    arriving = started(full_hbm, full, sems.at[0])
    tapping = started(feature_hbm.at[:, :, lanes], feature, sems.at[2])
    pace = rate[:, lanes]
    tapping.wait()
    taps = taps_of(feature)
    me = lax.axis_index(FAR)
    peers = full.shape[0]
    span = float(ROWS * peers)
    e_group = jnp.exp(-span * pace)
    g_first = jnp.exp(-(span - 1.0) * pace)
    g_second = jnp.exp(-(span - 2.0) * pace)
    e_block = jnp.exp(-float(ROWS) * pace)
    e_first = jnp.exp(-float(ROWS - 1) * pace)
    e_second = jnp.exp(-float(ROWS - 2) * pace)
    carry = jnp.zeros_like(pace)
    before = jnp.zeros((4, pace.shape[1]), F32)
    own0 = jnp.zeros((1, pace.shape[1]), F32)
    own1 = own0
    for i in range(came.shape[0]):
        block = came[i].astype(F32)
        u0, u1 = first_two(taps, block[16:20], before)
        before = block[20:24]
        total = block[0:MODES] + g_first * u0 + g_second * u1
        carry = jnp.where(i < me, e_group * carry + total, carry)
        own0 = jnp.where(i == me, u0, own0)
        own1 = jnp.where(i == me, u1, own1)
    arriving.wait()
    out[0] = carry
    carry = e_block * carry + (full[0] + e_first * own0 + e_second * own1)
    for i in range(1, peers):
        out[i] = carry
        carry = e_block * carry + full[i]
    started(out, out_hbm, sems.at[1]).wait()


def reach_kernel(rate, weight, out):
    place = (lax.broadcasted_iota(jnp.int32, (HALF, LANES), 0) + 1).astype(F32)

    def block(index):
        lanes = lanes_at(index)
        for m in range(MODES):
            out[m, :, lanes] = weight[m : m + 1, lanes] * jnp.exp(-place * rate[m : m + 1, lanes])

    over(rate.shape[1] // LANES, block)


def fill_lags(reach, rate, lags):
    def block(index):
        lanes = lanes_at(index)
        pace = rate[:, lanes]
        far = jnp.exp(-float(HALF) * pace)
        back = jnp.exp(pace)
        low = jnp.zeros((HALF, LANES), F32)
        high = low
        now = jnp.zeros((1, LANES), F32)
        for m in range(MODES):
            tap = reach[m, :, lanes]
            low = low + tap
            high = high + tap * far[m : m + 1]
            now = now + tap[0:1] * back[m : m + 1]
        lags[0:HALF, lanes] = low
        lags[HALF:STEP, lanes] = high
        lags[STEP - 1 : STEP, lanes] = now

    over(rate.shape[1] // LANES, block)


def add_modes(low, high, reach, rows, slot, lanes):
    for m in range(MODES):
        near = reach[m, :, lanes]
        far = near * rows[slot, GROUPS * MODES + m : GROUPS * MODES + m + 1]
        for g in range(GROUPS):
            state = rows[slot, g * MODES + m : g * MODES + m + 1]
            low[g] = low[g] + near * state
            high[g] = high[g] + far * state


SHORT_PIECES = 4


def short_kernel(
    gate_hbm, key_hbm, value_hbm, rim_hbm, feature_hbm, taps_hbm, out_hbm, gate, key, value, rim, feature, taps, out, kw, vw, gw, uw, sems, outs
):
    width = key.shape[1]

    def large(index):
        span = piece(width, SHORT_PIECES, index)
        return [
            pltpu.make_async_copy(a.at[:, span], b.at[:, span], sems.at[3 + 3 * index + j])
            for j, (a, b) in enumerate(((gate_hbm, gate), (key_hbm, key), (value_hbm, value)))
        ]

    def leaving(index):
        span = piece(width, SHORT_PIECES, index)
        return pltpu.make_async_copy(out.at[:, span], out_hbm.at[:, span], outs.at[index])

    small = [
        started(rim_hbm, rim, sems.at[0]),
        started(feature_hbm, feature, sems.at[1]),
        started(taps_hbm, taps, sems.at[2]),
    ]
    for index in range(SHORT_PIECES):
        for copy in large(index):
            copy.start()
    for slot in range(2):
        kw[slot, 0:8] = jnp.zeros((8, LANES), F32)
        vw[slot, 0:8] = jnp.zeros((8, LANES), F32)
        gw[slot, 0:16] = jnp.zeros((16, LANES), F32)
    for copy in small:
        copy.wait()

    def one(block, slot):
        lanes = lanes_at(block)
        halo = rim[:, lanes].astype(F32)
        kw[slot, 8:16] = halo[0:8]
        kw[slot, 16 : 16 + ROWS] = key[:, lanes].astype(F32)
        vw[slot, 8:16] = halo[8:16]
        vw[slot, 16 : 16 + ROWS] = value[:, lanes].astype(F32)
        gw[slot, 14:16] = halo[16:18]
        gw[slot, 16 : 16 + ROWS] = gate[:, lanes].astype(F32)

        def feat(w, stream, start, count):
            f = [feature[j, stream : stream + 1, lanes] for j in range(3)]
            return (
                f[0] * w[slot, start : start + count]
                + f[1] * w[slot, start - 1 : start - 1 + count]
                + f[2] * w[slot, start - 2 : start - 2 + count]
            )

        u = feat(kw, 1, 8, ROWS + 8) * feat(vw, 2, 8, ROWS + 8)
        uw[slot] = u.astype(BF16).astype(F32)
        mixed = taps[0:1, lanes] * uw[slot, 8 : 8 + ROWS]
        for lag in range(1, taps.shape[0]):
            mixed = mixed + taps[lag : lag + 1, lanes] * uw[slot, 8 - lag : 8 - lag + ROWS]
        out[:, lanes] = (feat(gw, 0, 16, ROWS) * mixed).astype(BF16)

    each = width // SHORT_PIECES // LANES // 2

    def some(index):
        for copy in large(index):
            copy.wait()

        def pair(inner):
            for slot in range(2):
                one((index * each + inner) * 2 + slot, slot)

        over(each, pair)
        leaving(index).start()

    over(SHORT_PIECES, some)
    for index in range(SHORT_PIECES):
        leaving(index).wait()


LOCAL_PIECES = 4


def local_kernel(
    gate_hbm, key_hbm, value_hbm, rim_hbm, feature_hbm, skip_hbm, kept_hbm, reach, rate, out, gate, key, value, rim, feature, skip, lags, kept, kw, vw, gw, uw, rows, sems
):
    width = key.shape[1]

    def large(index):
        span = piece(width, LOCAL_PIECES, index)
        pairs = ((gate_hbm, gate), (key_hbm, key), (value_hbm, value))
        return [
            pltpu.make_async_copy(a.at[:, span], b.at[:, span], sems.at[4 + 4 * index + j]) for j, (a, b) in enumerate(pairs)
        ] + [pltpu.make_async_copy(kept_hbm.at[:, :, span], kept.at[:, :, span], sems.at[7 + 4 * index])]

    small = [
        started(rim_hbm, rim, sems.at[0]),
        started(feature_hbm, feature, sems.at[1]),
        started(skip_hbm, skip, sems.at[2]),
    ]
    for index in range(LOCAL_PIECES):
        for copy in large(index):
            copy.start()
    for w in (kw, vw, gw, uw):
        for slot in range(2):
            w[slot, 0:16] = jnp.zeros((16, LANES), F32)
    place = lax.broadcasted_iota(jnp.int32, (STEP, LANES), 0)
    fill_lags(reach, rate, lags)
    for copy in small:
        copy.wait()

    def one(block, slot):
        lanes = lanes_at(block)
        halo = rim[:, lanes].astype(F32)
        kw[slot, 14:16] = halo[18:20]
        kw[slot, 16 : 16 + ROWS] = key[:, lanes].astype(F32)
        vw[slot, 14:16] = halo[20:22]
        vw[slot, 16 : 16 + ROWS] = value[:, lanes].astype(F32)
        gw[slot, 14:16] = halo[22:24]
        gw[slot, 16 : 16 + ROWS] = gate[:, lanes].astype(F32)

        def feat(w, stream):
            f = [feature[j, stream : stream + 1, lanes] for j in range(3)]
            return f[0] * w[slot, 16 : 16 + ROWS] + f[1] * w[slot, 15 : 15 + ROWS] + f[2] * w[slot, 14 : 14 + ROWS]

        out[ROWS : 2 * ROWS, lanes] = feat(gw, 0)
        uw[slot, 16 : 16 + ROWS] = (feat(kw, 1) * feat(vw, 2)).astype(BF16).astype(F32)
        pace = rate[:, lanes]
        jump = jnp.exp(-float(STEP) * pace)
        state = uw[slot, 16:17] * jnp.exp(-float(STEP - 1) * pace) + uw[slot, 17:18] * jnp.exp(-float(STEP - 2) * pace)
        rows[slot, 0:MODES] = jnp.zeros((MODES, LANES), F32)
        for g in range(1, GROUPS):
            rows[slot, g * MODES : (g + 1) * MODES] = kept[g, :, lanes] + state
            state = state * jump
        rows[slot, GROUPS * MODES : (GROUPS + 1) * MODES] = jnp.exp(-float(HALF) * pace)
        now = lags[STEP - 1 : STEP, lanes] + skip[:, lanes]
        low, high = [], []
        for g in range(GROUPS):
            start = 16 + g * STEP
            low.append(now * uw[slot, start : start + HALF])
            high.append(now * uw[slot, start + HALF : start + STEP])
        for lag in range(1, STEP):
            tap = jnp.where(place >= lag, lags[lag - 1 : lag, lanes], 0.0)
            for g in range(GROUPS):
                start = 16 + g * STEP - lag
                if lag < HALF:
                    low[g] = low[g] + tap[0:HALF] * uw[slot, start : start + HALF]
                high[g] = high[g] + tap[HALF:STEP] * uw[slot, start + HALF : start + STEP]
        add_modes(low, high, reach, rows, slot, lanes)
        for g in range(GROUPS):
            out[g * STEP : g * STEP + HALF, lanes] = low[g]
            out[g * STEP + HALF : (g + 1) * STEP, lanes] = high[g]

    each = width // LOCAL_PIECES // LANES // 2
    for index in range(LOCAL_PIECES):
        for copy in large(index):
            copy.wait()

        def pair(inner):
            for slot in range(2):
                one((index * each + inner) * 2 + slot, slot)

        over(each, pair)


FINISH_PIECES = 4


def finish_kernel(came, local, reach, rate, out_hbm, out, rows, outs):
    width = rate.shape[1]

    def leaving(index):
        span = piece(width, FINISH_PIECES, index)
        return pltpu.make_async_copy(out.at[:, span], out_hbm.at[:, span], outs.at[index])

    each = width // FINISH_PIECES // LANES // 2

    def one(owner, slot):
        lanes = lanes_at(owner * 2 + slot)
        state = came[owner, :, slot * LANES : (slot + 1) * LANES]
        pace = rate[:, lanes]
        jump = jnp.exp(-float(STEP) * pace)
        for g in range(GROUPS):
            rows[slot, g * MODES : (g + 1) * MODES] = state
            state = state * jump
        rows[slot, GROUPS * MODES : (GROUPS + 1) * MODES] = jnp.exp(-float(HALF) * pace)
        low = [local[g * STEP : g * STEP + HALF, lanes] for g in range(GROUPS)]
        high = [local[g * STEP + HALF : (g + 1) * STEP, lanes] for g in range(GROUPS)]
        add_modes(low, high, reach, rows, slot, lanes)
        for g in range(GROUPS):
            total = local[ROWS + g * STEP : ROWS + (g + 1) * STEP, lanes] * jnp.concatenate([low[g], high[g]], axis=0)
            out[g * STEP : (g + 1) * STEP, lanes] = total.astype(BF16)

    def some(index):
        def pair(inner):
            for slot in range(2):
                one(index * each + inner, slot)

        over(each, pair)
        leaving(index).start()

    over(FINISH_PIECES, some)
    for index in range(FINISH_PIECES):
        leaving(index).wait()


def shards(
    se_gate,
    se_key,
    se_value,
    li_gate,
    li_key,
    li_value,
    se_feature,
    se_filter,
    li_feature,
    li_residue,
    li_rate,
    li_skip,
):
    width = se_gate.shape[1]
    chips = lax.axis_size("chip")
    near = lax.axis_size(NEAR)
    far = lax.axis_size(FAR)
    part = width // near
    swap = lambda value, axis: lax.all_to_all(value, axis, split_axis=0, concat_axis=0, tiled=True)
    dma = pltpu.SemaphoreType.DMA
    stream = room(ROWS, width, dtype=BF16)
    padded = room(2, 16 + ROWS, LANES)
    rim_room = room(32, width, dtype=BF16)
    feature_room = room(*li_feature.shape)

    kept, sent = call(
        states_kernel,
        "states",
        [HBM] * 4,
        [(slow(GROUPS, MODES, width), HBM), (slow(near, 24, part), HBM)],
        [
            stream,
            stream,
            feature_room,
            room(MODES, width),
            room(GROUPS, MODES, width),
            room(near, 24, part),
            room(2, 3, 8 + ROWS, LANES),
            room(CHUNK, ROWS, LANES),
            dma((2 + 2 * (width // (CHUNK * LANES)),)),
            dma((2 * (width // (CHUNK * LANES)),)),
        ],
        12000000,
        3000000,
    )(li_key, li_value, li_feature, li_rate)

    came = swap(sent, NEAR)
    rim = call(
        rim_kernel,
        "rim",
        [HBM] * 7,
        [(fast(32, width, dtype=BF16), AUTO)],
        [room(6, 16, width, dtype=BF16), room(32, width), dma((6,))],
        1000000,
        500000,
    )(se_gate, se_key, se_value, li_gate, li_key, li_value, kept)
    weight = li_residue * jnp.sqrt(-jnp.expm1(-2.0 * li_rate))
    reach = call(
        reach_kernel, "reach", [AUTO] * 2, [(fast(MODES, HALF, width), AUTO)], [], 3000000, 2000000
    )(li_rate, weight)
    came, reach = lax.optimization_barrier((came, reach))

    group, full = call(
        functools.partial(group_kernel, chips),
        "group",
        [AUTO] * 3,
        [(slow(far, 24, part, dtype=BF16), HBM), (slow(near, MODES, part), HBM)],
        [room(24, part, dtype=BF16), room(near, MODES, part), dma((far + 1,))],
        500000,
        500000,
    )(came, li_feature, li_rate)

    groups = swap(group, FAR)
    count = lax.axis_size(PART)
    halo = lax.ppermute(rim, PART, [(i, i + 1) for i in range(count - 1)])
    local = call(
        local_kernel,
        "local",
        [HBM] * 7 + [AUTO] * 2,
        [(fast(2 * ROWS, width), AUTO)],
        [
            stream,
            stream,
            stream,
            rim_room,
            feature_room,
            room(1, width),
            room(STEP, width),
            room(GROUPS, MODES, width),
            padded,
            padded,
            padded,
            padded,
            room(2, (GROUPS + 1) * MODES, LANES),
            dma((4 + 4 * LOCAL_PIECES,)),
        ],
        LOCAL_FLOPS,
        3000000,
    )(li_gate, li_key, li_value, halo, li_feature, li_skip.reshape(1, width), kept, reach, li_rate)

    groups, local = lax.optimization_barrier((groups, local))

    states = call(
        functools.partial(carry_kernel, chips),
        "carry",
        [AUTO, HBM, HBM, AUTO],
        [(slow(near, MODES, part), HBM)],
        [room(near, MODES, part), room(near, MODES, part), room(3, 3, part), dma((3,))],
        500000,
        500000,
    )(groups, full, li_feature, li_rate)

    back = swap(states, NEAR)
    se_out = call(
        short_kernel,
        "short",
        [HBM] * 6,
        [(slow(ROWS, width, dtype=BF16), HBM)],
        [
            stream,
            stream,
            stream,
            rim_room,
            feature_room,
            room(*se_filter.shape),
            stream,
            padded,
            padded,
            padded,
            room(2, 8 + ROWS, LANES),
            dma((3 + 3 * SHORT_PIECES,)),
            dma((SHORT_PIECES,)),
        ],
        12000000,
        2000000,
    )(se_gate, se_key, se_value, halo, se_feature, se_filter)
    li_out = call(
        finish_kernel,
        "finish",
        [AUTO] * 4,
        [(slow(ROWS, width, dtype=BF16), HBM)],
        [stream, room(2, (GROUPS + 1) * MODES, LANES), dma((FINISH_PIECES,))],
        10000000,
        5000000,
    )(back, local, reach, li_rate)
    return (se_out, li_out)


def solution(mesh):
    sizes = dict(zip(mesh.axis_names, mesh.devices.shape))
    split = mesh.devices.reshape(sizes["dp"], sizes["node"] // 2, 2, sizes["chip"])
    inner = Mesh(split, ("dp", "far", "core", "chip"))
    rows = P(("dp", "far", "core", "chip"), None)
    return jax.shard_map(
        shards,
        mesh=inner,
        in_specs=(rows,) * 6 + (P(),) * 6,
        out_specs=(rows, rows),
        check_vma=False,
    )
```

```python
import functools

import jax
import jax.numpy as jnp
from jax import lax
from jax.experimental import pallas as pl
from jax.experimental.pallas import tpu as pltpu
from jax.sharding import Mesh, PartitionSpec as P

F32 = jnp.float32
BF16 = jnp.bfloat16
LANES = 128
NEAR = ("core", "chip")
FAR = "far"
PART = ("far", "core", "chip")
ROWS = 128
STEP = 16
GROUPS = ROWS // STEP
HALF = STEP // 2
MODES = 16
VMEM_LIMIT = 16 * 1024 * 1024
HBM = pl.BlockSpec(memory_space=pltpu.HBM)
AUTO = None


LOCAL_FLOPS = 50_000_000_000

def fast(*dims, dtype=F32):
    return pltpu.VMEM(dims, dtype)


def shape(*dims, dtype=F32):
    return jax.ShapeDtypeStruct(dims, dtype)


def slow(*dims, dtype=F32):
    return pltpu.HBM(dims, dtype)


def room(*dims, dtype=F32):
    return pltpu.VMEM(dims, dtype)


def call(kernel, name, ins, outs, scratch, flops, moved):
    whole = lambda spec: pl.BlockSpec(memory_space=pltpu.VMEM) if spec is None else spec
    many = len(outs) > 1
    inner = pl.pallas_call(
        kernel,
        out_shape=tuple(o for o, _ in outs) if many else outs[0][0],
        in_specs=[whole(spec) for spec in ins],
        out_specs=tuple(whole(spec) for _, spec in outs) if many else whole(outs[0][1]),
        name=name,
        scratch_shapes=list(scratch),
        compiler_params=pltpu.CompilerParams(vmem_limit_bytes=VMEM_LIMIT),
        cost_estimate=pl.CostEstimate(flops=flops, bytes_accessed=moved, transcendentals=0),
    )

    def outer(*values):
        return inner(
            *[pltpu.with_memory_space_constraint(v, pltpu.HBM) if spec is HBM else v for v, spec in zip(values, ins)]
        )

    return outer


def lanes_at(index):
    return pl.ds(pl.multiple_of(index * LANES, LANES), LANES)


def started(source, target, semaphore):
    copy = pltpu.make_async_copy(source, target, semaphore)
    copy.start()
    return copy


def piece(width, count, index):
    size = width // count
    return pl.ds(pl.multiple_of(index * size, size), size)


def over(count, body):
    lax.fori_loop(0, count, lambda index, carry: body(index) or carry, 0)


def fill_rim(tails, key, value, held, out):
    held[0:8] = tails[1].astype(F32)[8:16]
    held[8:16] = tails[2].astype(F32)[8:16]
    held[16:18] = tails[0].astype(F32)[14:16]
    held[18:20] = key[ROWS - 16 : ROWS].astype(F32)[14:16]
    held[20:22] = value[ROWS - 16 : ROWS].astype(F32)[14:16]
    held[22:24] = tails[3].astype(F32)[14:16]
    held[24:32] = jnp.zeros_like(held[24:32])
    out[...] = held[...].astype(BF16)


def rim_kernel(rim, out):
    out[...] = rim[...]


CHUNK = 4


def states_kernel(
    key_hbm, value_hbm, feature_hbm, rate_hbm, seg, sek, sev, lig, kept_hbm, sent_hbm, rim, key, value, feature, rate, kept, sent, packed, wide, fresh, tails, held, sems, outs, tail_sems
):
    width = key.shape[1]
    chunks = width // (CHUNK * LANES)

    def large(index):
        span = piece(width, chunks, index)
        return [
            pltpu.make_async_copy(key_hbm.at[:, span], key.at[:, span], sems.at[2 + 2 * index]),
            pltpu.make_async_copy(value_hbm.at[:, span], value.at[:, span], sems.at[3 + 2 * index]),
        ]

    def leaving(index):
        span = piece(width, chunks, index)
        owners = pl.ds(index * (CHUNK // 2), CHUNK // 2)
        return [
            pltpu.make_async_copy(packed.at[owners], sent_hbm.at[owners], outs.at[2 * index]),
            pltpu.make_async_copy(kept.at[:, :, span], kept_hbm.at[:, :, span], outs.at[2 * index + 1]),
        ]

    for copy in large(0):
        copy.start()
    small = [started(feature_hbm, feature, sems.at[0]), started(rate_hbm, rate, sems.at[1])]
    for index in range(1, chunks):
        for copy in large(index):
            copy.start()
    last = [started(ref.at[ROWS - 16 : ROWS], tails.at[i], tail_sems.at[i]) for i, ref in enumerate((seg, sek, sev, lig))]
    for copy in small:
        copy.wait()

    def featurized(ref, stream, lanes, slot):
        raw = ref[:, lanes].astype(F32)
        wide[slot, stream, 8 : 8 + ROWS] = raw
        return (
            feature[0, stream : stream + 1, lanes] * raw
            + feature[1, stream : stream + 1, lanes] * wide[slot, stream, 7 : 7 + ROWS]
            + feature[2, stream : stream + 1, lanes] * wide[slot, stream, 6 : 6 + ROWS]
        )

    wide[:, :, 0:8] = jnp.zeros((2, 3, 8, LANES), F32)

    def chunk(index):
        for copy in large(index):
            copy.wait()
        decays = []
        for part in range(CHUNK):
            block = index * CHUNK + part
            lanes = lanes_at(block)
            owner = index * (CHUNK // 2) + part // 2
            half = slice((part % 2) * LANES, (part % 2 + 1) * LANES)
            slot = part % 2
            u = featurized(key, 1, lanes, slot) * featurized(value, 2, lanes, slot)
            fresh[part] = u.astype(BF16).astype(F32)
            fresh[part, 0:2] = jnp.zeros((2, LANES), F32)
            sent[owner, 16:18, half] = wide[slot, 1, 8:10]
            sent[owner, 18:20, half] = wide[slot, 2, 8:10]
            sent[owner, 20:22, half] = wide[slot, 1, ROWS + 6 : ROWS + 8]
            sent[owner, 22:24, half] = wide[slot, 2, ROWS + 6 : ROWS + 8]
            decays.append([jnp.exp(-times * rate[:, lanes]) for times in (1.0, 2.0, 4.0)])
        states = [jnp.zeros((MODES, LANES), F32)] * CHUNK
        for t in range(0, ROWS, 4):
            for part in range(CHUNK):
                if t % STEP == 0:
                    kept[t // STEP, :, lanes_at(index * CHUNK + part)] = states[part]
                row = [fresh[part, t + i : t + i + 1, :] for i in range(4)]
                one, two, four = decays[part]
                first = one * row[0] + row[1]
                second = one * row[2] + row[3]
                states[part] = four * states[part] + (two * first + second)
        for part in range(CHUNK):
            half = slice((part % 2) * LANES, (part % 2 + 1) * LANES)
            sent[index * (CHUNK // 2) + part // 2, 0:MODES, half] = states[part]
        for owner in range(CHUNK // 2):
            packed[index * (CHUNK // 2) + owner] = sent[index * (CHUNK // 2) + owner].astype(BF16)
        for copy in leaving(index):
            copy.start()

    over(chunks, chunk)
    for copy in last:
        copy.wait()
    fill_rim(tails, key, value, held, rim)
    for index in range(chunks):
        for copy in leaving(index):
            copy.wait()


def first_two(taps, own, before):
    row = lax.broadcasted_iota(jnp.int32, own.shape, 0)
    two = pltpu.roll(before, 4, 0)
    one = jnp.where(row % 2 == 0, pltpu.roll(two, 7, 0), pltpu.roll(own, 1, 0))
    featurized = taps[0] * own + taps[1] * one + taps[2] * two
    u = (featurized * pltpu.roll(featurized, 6, 0)).astype(BF16).astype(F32)
    return u[0:1], u[1:2]


def owned_lanes(chips, width):
    me = lax.axis_index("core") * chips + lax.axis_index("chip")
    return pl.ds(pl.multiple_of(me * width, width), width)


def taps_of(feature):
    width = feature.shape[2]
    row = lax.broadcasted_iota(jnp.int32, (8, width), 0)
    return [jnp.where(row < 2, feature[j, 1:2], feature[j, 2:3]) for j in range(3)]


def group_kernel(chips, came, feature, rate, sent_hbm, full_hbm, own, sent, full, sems):
    lanes = owned_lanes(chips, came.shape[2])
    own[...] = feature[:, :, lanes]
    taps = taps_of(own)
    pace = rate[:, lanes]
    e_block = jnp.exp(-float(ROWS) * pace)
    e_first = jnp.exp(-float(ROWS - 1) * pace)
    e_second = jnp.exp(-float(ROWS - 2) * pace)
    peers = came.shape[0]
    blocks = [came[i].astype(F32) for i in range(peers)]
    total = blocks[0][0:MODES]
    full[0] = total
    for i in range(1, peers):
        u0, u1 = first_two(taps, blocks[i][16:24], blocks[i - 1][16:24])
        mine = blocks[i][0:MODES] + e_first * u0 + e_second * u1
        full[i] = mine
        total = e_block * total + mine
    row = lax.broadcasted_iota(jnp.int32, (8, came.shape[2]), 0)
    rims = jnp.where(row < 4, blocks[0][16:24], blocks[peers - 1][16:24])
    sent[...] = jnp.concatenate([total, rims], axis=0).astype(BF16)
    copies = [started(sent, sent_hbm.at[i], sems.at[i]) for i in range(sent_hbm.shape[0])]
    copies.append(started(full, full_hbm, sems.at[sent_hbm.shape[0]]))
    for copy in copies:
        copy.wait()


def carry_kernel(chips, came, full_hbm, feature, rate, out_hbm, full, out, sems):
    lanes = owned_lanes(chips, came.shape[2])
    arriving = started(full_hbm, full, sems.at[0])
    pace = rate[:, lanes]
    taps = taps_of(feature)
    me = lax.axis_index(FAR)
    peers = full.shape[0]
    span = float(ROWS * peers)
    e_group = jnp.exp(-span * pace)
    g_first = jnp.exp(-(span - 1.0) * pace)
    g_second = jnp.exp(-(span - 2.0) * pace)
    e_block = jnp.exp(-float(ROWS) * pace)
    e_first = jnp.exp(-float(ROWS - 1) * pace)
    e_second = jnp.exp(-float(ROWS - 2) * pace)
    carry = jnp.zeros_like(pace)
    before = jnp.zeros((8, pace.shape[1]), F32)
    own0 = jnp.zeros((1, pace.shape[1]), F32)
    own1 = own0
    for i in range(came.shape[0]):
        block = came[i].astype(F32)
        u0, u1 = first_two(taps, block[16:24], before)
        before = block[16:24]
        total = block[0:MODES] + g_first * u0 + g_second * u1
        carry = jnp.where(i < me, e_group * carry + total, carry)
        own0 = jnp.where(i == me, u0, own0)
        own1 = jnp.where(i == me, u1, own1)
    arriving.wait()
    out[0] = carry.astype(BF16)
    carry = e_block * carry + (full[0] + e_first * own0 + e_second * own1)
    for i in range(1, peers):
        out[i] = carry.astype(BF16)
        carry = e_block * carry + full[i]
    started(out, out_hbm, sems.at[1]).wait()


def reach_kernel(rate, weight, out):
    place = (lax.broadcasted_iota(jnp.int32, (HALF, LANES), 0) + 1).astype(F32)

    def block(index):
        lanes = lanes_at(index)
        for m in range(MODES):
            out[m, :, lanes] = weight[m : m + 1, lanes] * jnp.exp(-place * rate[m : m + 1, lanes])

    over(rate.shape[1] // LANES, block)


def fill_lags(reach, rate, lags):
    def block(index):
        lanes = lanes_at(index)
        pace = rate[:, lanes]
        far = jnp.exp(-float(HALF) * pace)
        back = jnp.exp(pace)
        low = jnp.zeros((HALF, LANES), F32)
        high = low
        now = jnp.zeros((1, LANES), F32)
        for m in range(MODES):
            tap = reach[m, :, lanes]
            low = low + tap
            high = high + tap * far[m : m + 1]
            now = now + tap[0:1] * back[m : m + 1]
        lags[0:HALF, lanes] = low
        lags[HALF:STEP, lanes] = high
        lags[STEP - 1 : STEP, lanes] = now

    over(rate.shape[1] // LANES, block)


def add_modes(low, high, reach, rows, slot, lanes):
    for m in range(MODES):
        near = reach[m, :, lanes]
        far = near * rows[slot, GROUPS * MODES + m : GROUPS * MODES + m + 1]
        for g in range(GROUPS):
            state = rows[slot, g * MODES + m : g * MODES + m + 1]
            low[g] = low[g] + near * state
            high[g] = high[g] + far * state


SHORT_PIECES = 4


def short_kernel(
    gate_hbm, key_hbm, value_hbm, rim_hbm, feature_hbm, taps_hbm, out_hbm, gate, key, value, rim, feature, taps, out, kw, vw, gw, uw, sems, outs
):
    width = key.shape[1]

    def large(index):
        span = piece(width, SHORT_PIECES, index)
        return [
            pltpu.make_async_copy(a.at[:, span], b.at[:, span], sems.at[3 + 3 * index + j])
            for j, (a, b) in enumerate(((gate_hbm, gate), (key_hbm, key), (value_hbm, value)))
        ]

    def leaving(index):
        span = piece(width, SHORT_PIECES, index)
        return pltpu.make_async_copy(out.at[:, span], out_hbm.at[:, span], outs.at[index])

    small = [
        started(rim_hbm, rim, sems.at[0]),
        started(feature_hbm, feature, sems.at[1]),
        started(taps_hbm, taps, sems.at[2]),
    ]
    for index in range(SHORT_PIECES):
        for copy in large(index):
            copy.start()
    for slot in range(2):
        kw[slot, 0:8] = jnp.zeros((8, LANES), F32)
        vw[slot, 0:8] = jnp.zeros((8, LANES), F32)
        gw[slot, 0:16] = jnp.zeros((16, LANES), F32)
    for copy in small:
        copy.wait()

    def one(block, slot):
        lanes = lanes_at(block)
        halo = rim[:, lanes].astype(F32)
        kw[slot, 8:16] = halo[0:8]
        kw[slot, 16 : 16 + ROWS] = key[:, lanes].astype(F32)
        vw[slot, 8:16] = halo[8:16]
        vw[slot, 16 : 16 + ROWS] = value[:, lanes].astype(F32)
        gw[slot, 14:16] = halo[16:18]
        gw[slot, 16 : 16 + ROWS] = gate[:, lanes].astype(F32)

        def feat(w, stream, start, count):
            f = [feature[j, stream : stream + 1, lanes] for j in range(3)]
            return (
                f[0] * w[slot, start : start + count]
                + f[1] * w[slot, start - 1 : start - 1 + count]
                + f[2] * w[slot, start - 2 : start - 2 + count]
            )

        u = feat(kw, 1, 8, ROWS + 8) * feat(vw, 2, 8, ROWS + 8)
        uw[slot] = u.astype(BF16).astype(F32)
        mixed = taps[0:1, lanes] * uw[slot, 8 : 8 + ROWS]
        for lag in range(1, taps.shape[0]):
            mixed = mixed + taps[lag : lag + 1, lanes] * uw[slot, 8 - lag : 8 - lag + ROWS]
        out[:, lanes] = (feat(gw, 0, 16, ROWS) * mixed).astype(BF16)

    each = width // SHORT_PIECES // LANES // 2

    def some(index):
        for copy in large(index):
            copy.wait()

        def pair(inner):
            for slot in range(2):
                one((index * each + inner) * 2 + slot, slot)

        over(each, pair)
        leaving(index).start()

    over(SHORT_PIECES, some)
    for index in range(SHORT_PIECES):
        leaving(index).wait()


LOCAL_PIECES = 4


def local_kernel(
    gate_hbm, key_hbm, value_hbm, rim_hbm, feature_hbm, skip_hbm, kept_hbm, reach, rate, out, gate, key, value, rim, feature, skip, lags, kept, kw, vw, gw, uw, rows, sems
):
    width = key.shape[1]

    def large(index):
        span = piece(width, LOCAL_PIECES, index)
        pairs = ((gate_hbm, gate), (key_hbm, key), (value_hbm, value))
        return [
            pltpu.make_async_copy(a.at[:, span], b.at[:, span], sems.at[4 + 4 * index + j]) for j, (a, b) in enumerate(pairs)
        ] + [pltpu.make_async_copy(kept_hbm.at[:, :, span], kept.at[:, :, span], sems.at[7 + 4 * index])]

    small = [
        started(rim_hbm, rim, sems.at[0]),
        started(feature_hbm, feature, sems.at[1]),
        started(skip_hbm, skip, sems.at[2]),
    ]
    for index in range(LOCAL_PIECES):
        for copy in large(index):
            copy.start()
    for w in (kw, vw, gw, uw):
        for slot in range(2):
            w[slot, 0:16] = jnp.zeros((16, LANES), F32)
    place = lax.broadcasted_iota(jnp.int32, (STEP, LANES), 0)
    fill_lags(reach, rate, lags)
    for copy in small:
        copy.wait()

    def one(block, slot):
        lanes = lanes_at(block)
        halo = rim[:, lanes].astype(F32)
        kw[slot, 14:16] = halo[18:20]
        kw[slot, 16 : 16 + ROWS] = key[:, lanes].astype(F32)
        vw[slot, 14:16] = halo[20:22]
        vw[slot, 16 : 16 + ROWS] = value[:, lanes].astype(F32)
        gw[slot, 14:16] = halo[22:24]
        gw[slot, 16 : 16 + ROWS] = gate[:, lanes].astype(F32)

        def feat(w, stream):
            f = [feature[j, stream : stream + 1, lanes] for j in range(3)]
            return f[0] * w[slot, 16 : 16 + ROWS] + f[1] * w[slot, 15 : 15 + ROWS] + f[2] * w[slot, 14 : 14 + ROWS]

        out[ROWS : 2 * ROWS, lanes] = feat(gw, 0)
        uw[slot, 16 : 16 + ROWS] = (feat(kw, 1) * feat(vw, 2)).astype(BF16).astype(F32)
        pace = rate[:, lanes]
        jump = jnp.exp(-float(STEP) * pace)
        state = uw[slot, 16:17] * jnp.exp(-float(STEP - 1) * pace) + uw[slot, 17:18] * jnp.exp(-float(STEP - 2) * pace)
        rows[slot, 0:MODES] = jnp.zeros((MODES, LANES), F32)
        for g in range(1, GROUPS):
            rows[slot, g * MODES : (g + 1) * MODES] = kept[g, :, lanes] + state
            state = state * jump
        rows[slot, GROUPS * MODES : (GROUPS + 1) * MODES] = jnp.exp(-float(HALF) * pace)
        now = lags[STEP - 1 : STEP, lanes] + skip[:, lanes]
        low, high = [], []
        for g in range(GROUPS):
            start = 16 + g * STEP
            low.append(now * uw[slot, start : start + HALF])
            high.append(now * uw[slot, start + HALF : start + STEP])
        for lag in range(1, STEP):
            tap = jnp.where(place >= lag, lags[lag - 1 : lag, lanes], 0.0)
            for g in range(GROUPS):
                start = 16 + g * STEP - lag
                if lag < HALF:
                    low[g] = low[g] + tap[0:HALF] * uw[slot, start : start + HALF]
                high[g] = high[g] + tap[HALF:STEP] * uw[slot, start + HALF : start + STEP]
        add_modes(low, high, reach, rows, slot, lanes)
        for g in range(GROUPS):
            out[g * STEP : g * STEP + HALF, lanes] = low[g]
            out[g * STEP + HALF : (g + 1) * STEP, lanes] = high[g]

    each = width // LOCAL_PIECES // LANES // 2
    for index in range(LOCAL_PIECES):
        for copy in large(index):
            copy.wait()

        def pair(inner):
            for slot in range(2):
                one((index * each + inner) * 2 + slot, slot)

        over(each, pair)


FINISH_PIECES = 4


def finish_kernel(came, local, reach, rate, out_hbm, out, rows, outs):
    width = rate.shape[1]

    def leaving(index):
        span = piece(width, FINISH_PIECES, index)
        return pltpu.make_async_copy(out.at[:, span], out_hbm.at[:, span], outs.at[index])

    each = width // FINISH_PIECES // LANES // 2

    def one(owner, slot):
        lanes = lanes_at(owner * 2 + slot)
        state = came[owner, :, slot * LANES : (slot + 1) * LANES].astype(F32)
        pace = rate[:, lanes]
        jump = jnp.exp(-float(STEP) * pace)
        for g in range(GROUPS):
            rows[slot, g * MODES : (g + 1) * MODES] = state
            state = state * jump
        rows[slot, GROUPS * MODES : (GROUPS + 1) * MODES] = jnp.exp(-float(HALF) * pace)
        low = [local[g * STEP : g * STEP + HALF, lanes] for g in range(GROUPS)]
        high = [local[g * STEP + HALF : (g + 1) * STEP, lanes] for g in range(GROUPS)]
        add_modes(low, high, reach, rows, slot, lanes)
        for g in range(GROUPS):
            total = local[ROWS + g * STEP : ROWS + (g + 1) * STEP, lanes] * jnp.concatenate([low[g], high[g]], axis=0)
            out[g * STEP : (g + 1) * STEP, lanes] = total.astype(BF16)

    def some(index):
        def pair(inner):
            for slot in range(2):
                one(index * each + inner, slot)

        over(each, pair)
        leaving(index).start()

    over(FINISH_PIECES, some)
    for index in range(FINISH_PIECES):
        leaving(index).wait()


def shards(
    se_gate,
    se_key,
    se_value,
    li_gate,
    li_key,
    li_value,
    se_feature,
    se_filter,
    li_feature,
    li_residue,
    li_rate,
    li_skip,
):
    width = se_gate.shape[1]
    chips = lax.axis_size("chip")
    near = lax.axis_size(NEAR)
    far = lax.axis_size(FAR)
    part = width // near
    swap = lambda value, axis: lax.all_to_all(value, axis, split_axis=0, concat_axis=0, tiled=True)
    dma = pltpu.SemaphoreType.DMA
    stream = room(ROWS, width, dtype=BF16)
    padded = room(2, 16 + ROWS, LANES)
    rim_room = room(32, width, dtype=BF16)
    feature_room = room(*li_feature.shape)

    kept, sent, rim = call(
        states_kernel,
        "states",
        [HBM] * 8,
        [(slow(GROUPS, MODES, width), HBM), (slow(near, 24, part, dtype=BF16), HBM), (fast(32, width, dtype=BF16), AUTO)],
        [
            stream,
            stream,
            feature_room,
            room(MODES, width),
            room(GROUPS, MODES, width),
            room(near, 24, part),
            room(near, 24, part, dtype=BF16),
            room(2, 3, 8 + ROWS, LANES),
            room(CHUNK, ROWS, LANES),
            room(4, 16, width, dtype=BF16),
            room(32, width),
            dma((2 + 2 * (width // (CHUNK * LANES)),)),
            dma((2 * (width // (CHUNK * LANES)),)),
            dma((4,)),
        ],
        12000000,
        3000000,
    )(li_key, li_value, li_feature, li_rate, se_gate, se_key, se_value, li_gate)

    came = swap(sent, NEAR)
    rim = call(rim_kernel, "rim", [AUTO], [(fast(32, width, dtype=BF16), AUTO)], [], 1000000, 500000)(rim)
    weight = li_residue * jnp.sqrt(-jnp.expm1(-2.0 * li_rate))
    reach = call(
        reach_kernel, "reach", [AUTO] * 2, [(fast(MODES, HALF, width), AUTO)], [], 3000000, 2000000
    )(li_rate, weight)
    came, reach = lax.optimization_barrier((came, reach))

    group, full, taps = call(
        functools.partial(group_kernel, chips),
        "group",
        [AUTO] * 3,
        [(slow(far, 24, part, dtype=BF16), HBM), (slow(near, MODES, part), HBM), (fast(3, 3, part), AUTO)],
        [room(24, part, dtype=BF16), room(near, MODES, part), dma((far + 1,))],
        500000,
        500000,
    )(came, li_feature, li_rate)

    groups = swap(group, FAR)
    count = lax.axis_size(PART)
    halo = lax.ppermute(rim, PART, [(i, i + 1) for i in range(count - 1)])
    local = call(
        local_kernel,
        "local",
        [HBM] * 7 + [AUTO] * 2,
        [(fast(2 * ROWS, width), AUTO)],
        [
            stream,
            stream,
            stream,
            rim_room,
            feature_room,
            room(1, width),
            room(STEP, width),
            room(GROUPS, MODES, width),
            padded,
            padded,
            padded,
            padded,
            room(2, (GROUPS + 1) * MODES, LANES),
            dma((4 + 4 * LOCAL_PIECES,)),
        ],
        LOCAL_FLOPS,
        3000000,
    )(li_gate, li_key, li_value, halo, li_feature, li_skip.reshape(1, width), kept, reach, li_rate)

    groups, local = lax.optimization_barrier((groups, local))

    states = call(
        functools.partial(carry_kernel, chips),
        "carry",
        [AUTO, HBM, AUTO, AUTO],
        [(slow(near, MODES, part, dtype=BF16), HBM)],
        [room(near, MODES, part), room(near, MODES, part, dtype=BF16), dma((2,))],
        500000,
        500000,
    )(groups, full, taps, li_rate)

    back = swap(states, NEAR)
    se_out = call(
        short_kernel,
        "short",
        [HBM] * 6,
        [(slow(ROWS, width, dtype=BF16), HBM)],
        [
            stream,
            stream,
            stream,
            rim_room,
            feature_room,
            room(*se_filter.shape),
            stream,
            padded,
            padded,
            padded,
            room(2, 8 + ROWS, LANES),
            dma((3 + 3 * SHORT_PIECES,)),
            dma((SHORT_PIECES,)),
        ],
        12000000,
        2000000,
    )(se_gate, se_key, se_value, halo, se_feature, se_filter)
    li_out = call(
        finish_kernel,
        "finish",
        [AUTO] * 4,
        [(slow(ROWS, width, dtype=BF16), HBM)],
        [stream, room(2, (GROUPS + 1) * MODES, LANES), dma((FINISH_PIECES,))],
        10000000,
        5000000,
    )(back, local, reach, li_rate)
    return (se_out, li_out)


def solution(mesh):
    sizes = dict(zip(mesh.axis_names, mesh.devices.shape))
    split = mesh.devices.reshape(sizes["dp"], sizes["node"] // 2, 2, sizes["chip"])
    inner = Mesh(split, ("dp", "far", "core", "chip"))
    rows = P(("dp", "far", "core", "chip"), None)
    return jax.shard_map(
        shards,
        mesh=inner,
        in_specs=(rows,) * 6 + (P(),) * 6,
        out_specs=(rows, rows),
        check_vma=False,
    )
```

```python
import functools

import jax
import jax.numpy as jnp
from jax import lax
from jax.experimental import pallas as pl
from jax.experimental.pallas import tpu as pltpu
from jax.sharding import Mesh, PartitionSpec as P

F32 = jnp.float32
BF16 = jnp.bfloat16
LANES = 128
NEAR = ("core", "chip")
FAR = "far"
PART = ("far", "core", "chip")
ROWS = 128
STEP = 16
GROUPS = ROWS // STEP
HALF = STEP // 2
MODES = 16
VMEM_LIMIT = 16 * 1024 * 1024
HBM = pl.BlockSpec(memory_space=pltpu.HBM)
AUTO = None


LOCAL_FLOPS = 50_000_000_000

def fast(*dims, dtype=F32):
    return pltpu.VMEM(dims, dtype)


def shape(*dims, dtype=F32):
    return jax.ShapeDtypeStruct(dims, dtype)


def slow(*dims, dtype=F32):
    return pltpu.HBM(dims, dtype)


def room(*dims, dtype=F32):
    return pltpu.VMEM(dims, dtype)


def call(kernel, name, ins, outs, scratch, flops, moved):
    whole = lambda spec: pl.BlockSpec(memory_space=pltpu.VMEM) if spec is None else spec
    many = len(outs) > 1
    inner = pl.pallas_call(
        kernel,
        out_shape=tuple(o for o, _ in outs) if many else outs[0][0],
        in_specs=[whole(spec) for spec in ins],
        out_specs=tuple(whole(spec) for _, spec in outs) if many else whole(outs[0][1]),
        name=name,
        scratch_shapes=list(scratch),
        compiler_params=pltpu.CompilerParams(vmem_limit_bytes=VMEM_LIMIT),
        cost_estimate=pl.CostEstimate(flops=flops, bytes_accessed=moved, transcendentals=0),
    )

    def outer(*values):
        return inner(
            *[pltpu.with_memory_space_constraint(v, pltpu.HBM) if spec is HBM else v for v, spec in zip(values, ins)]
        )

    return outer


def lanes_at(index):
    return pl.ds(pl.multiple_of(index * LANES, LANES), LANES)


def started(source, target, semaphore):
    copy = pltpu.make_async_copy(source, target, semaphore)
    copy.start()
    return copy


def piece(width, count, index):
    size = width // count
    return pl.ds(pl.multiple_of(index * size, size), size)


def over(count, body):
    lax.fori_loop(0, count, lambda index, carry: body(index) or carry, 0)


def fill_rim(tails, key, value, held, out):
    held[0:8] = tails[1].astype(F32)[8:16]
    held[8:16] = tails[2].astype(F32)[8:16]
    held[16:18] = tails[0].astype(F32)[14:16]
    held[18:20] = key[ROWS - 16 : ROWS].astype(F32)[14:16]
    held[20:22] = value[ROWS - 16 : ROWS].astype(F32)[14:16]
    held[22:24] = tails[3].astype(F32)[14:16]
    held[24:32] = jnp.zeros_like(held[24:32])
    out[...] = held[...].astype(BF16)


def rim_kernel(rim, out):
    out[...] = rim[...]


CHUNK = 4


def states_kernel(
    key_hbm, value_hbm, feature_hbm, rate_hbm, seg, sek, sev, lig, kept_hbm, sent_hbm, rim, key, value, feature, rate, kept, sent, packed, wide, fresh, tails, held, sems, outs, tail_sems
):
    width = key.shape[1]
    chunks = width // (CHUNK * LANES)

    def large(index):
        span = piece(width, chunks, index)
        return [
            pltpu.make_async_copy(key_hbm.at[:, span], key.at[:, span], sems.at[2 + 2 * index]),
            pltpu.make_async_copy(value_hbm.at[:, span], value.at[:, span], sems.at[3 + 2 * index]),
        ]

    def leaving(index):
        span = piece(width, chunks, index)
        owners = pl.ds(index * (CHUNK // 2), CHUNK // 2)
        return [
            pltpu.make_async_copy(packed.at[owners], sent_hbm.at[owners], outs.at[2 * index]),
            pltpu.make_async_copy(kept.at[:, :, span], kept_hbm.at[:, :, span], outs.at[2 * index + 1]),
        ]

    for copy in large(0):
        copy.start()
    small = [started(feature_hbm, feature, sems.at[0]), started(rate_hbm, rate, sems.at[1])]
    for index in range(1, chunks):
        for copy in large(index):
            copy.start()
    last = [started(ref.at[ROWS - 16 : ROWS], tails.at[i], tail_sems.at[i]) for i, ref in enumerate((seg, sek, sev, lig))]
    for copy in small:
        copy.wait()

    def featurized(ref, stream, lanes, slot):
        raw = ref[:, lanes].astype(F32)
        wide[slot, stream, 8 : 8 + ROWS] = raw
        return (
            feature[0, stream : stream + 1, lanes] * raw
            + feature[1, stream : stream + 1, lanes] * wide[slot, stream, 7 : 7 + ROWS]
            + feature[2, stream : stream + 1, lanes] * wide[slot, stream, 6 : 6 + ROWS]
        )

    wide[:, :, 0:8] = jnp.zeros((2, 3, 8, LANES), F32)

    def chunk(index):
        for copy in large(index):
            copy.wait()
        decays = []
        for part in range(CHUNK):
            block = index * CHUNK + part
            lanes = lanes_at(block)
            owner = index * (CHUNK // 2) + part // 2
            half = slice((part % 2) * LANES, (part % 2 + 1) * LANES)
            slot = part % 2
            u = featurized(key, 1, lanes, slot) * featurized(value, 2, lanes, slot)
            fresh[part] = u.astype(BF16).astype(F32)
            fresh[part, 0:2] = jnp.zeros((2, LANES), F32)
            sent[owner, 16:18, half] = wide[slot, 1, 8:10]
            sent[owner, 18:20, half] = wide[slot, 2, 8:10]
            sent[owner, 20:22, half] = wide[slot, 1, ROWS + 6 : ROWS + 8]
            sent[owner, 22:24, half] = wide[slot, 2, ROWS + 6 : ROWS + 8]
            decays.append([jnp.exp(-times * rate[:, lanes]) for times in (1.0, 2.0, 4.0)])
        states = [jnp.zeros((MODES, LANES), F32)] * CHUNK
        for t in range(0, ROWS, 4):
            for part in range(CHUNK):
                if t % STEP == 0:
                    kept[t // STEP, :, lanes_at(index * CHUNK + part)] = states[part]
                row = [fresh[part, t + i : t + i + 1, :] for i in range(4)]
                one, two, four = decays[part]
                first = one * row[0] + row[1]
                second = one * row[2] + row[3]
                states[part] = four * states[part] + (two * first + second)
        for part in range(CHUNK):
            half = slice((part % 2) * LANES, (part % 2 + 1) * LANES)
            sent[index * (CHUNK // 2) + part // 2, 0:MODES, half] = states[part]
        for owner in range(CHUNK // 2):
            packed[index * (CHUNK // 2) + owner] = sent[index * (CHUNK // 2) + owner].astype(BF16)
        for copy in leaving(index):
            copy.start()

    over(chunks, chunk)
    for copy in last:
        copy.wait()
    fill_rim(tails, key, value, held, rim)
    for index in range(chunks):
        for copy in leaving(index):
            copy.wait()


def first_two(taps, own, before):
    row = lax.broadcasted_iota(jnp.int32, own.shape, 0)
    two = pltpu.roll(before, 4, 0)
    one = jnp.where(row % 2 == 0, pltpu.roll(two, 7, 0), pltpu.roll(own, 1, 0))
    featurized = taps[0] * own + taps[1] * one + taps[2] * two
    u = (featurized * pltpu.roll(featurized, 6, 0)).astype(BF16).astype(F32)
    return u[0:1], u[1:2]


def owned_lanes(chips, width):
    me = lax.axis_index("core") * chips + lax.axis_index("chip")
    return pl.ds(pl.multiple_of(me * width, width), width)


def taps_of(feature):
    width = feature.shape[2]
    row = lax.broadcasted_iota(jnp.int32, (8, width), 0)
    return [jnp.where(row < 2, feature[j, 1:2], feature[j, 2:3]) for j in range(3)]


def group_kernel(chips, came, feature, rate, sent_hbm, full_hbm, own, sent, full, sems):
    lanes = owned_lanes(chips, came.shape[2])
    own[...] = feature[:, :, lanes]
    taps = taps_of(own)
    pace = rate[:, lanes]
    e_block = jnp.exp(-float(ROWS) * pace)
    e_first = jnp.exp(-float(ROWS - 1) * pace)
    e_second = jnp.exp(-float(ROWS - 2) * pace)
    peers = came.shape[0]
    blocks = [came[i].astype(F32) for i in range(peers)]
    total = blocks[0][0:MODES]
    full[0] = total
    for i in range(1, peers):
        u0, u1 = first_two(taps, blocks[i][16:24], blocks[i - 1][16:24])
        mine = blocks[i][0:MODES] + e_first * u0 + e_second * u1
        full[i] = mine
        total = e_block * total + mine
    row = lax.broadcasted_iota(jnp.int32, (8, came.shape[2]), 0)
    rims = jnp.where(row < 4, blocks[0][16:24], blocks[peers - 1][16:24])
    sent[...] = jnp.concatenate([total, rims], axis=0).astype(BF16)
    copies = [started(sent, sent_hbm.at[i], sems.at[i]) for i in range(sent_hbm.shape[0])]
    copies.append(started(full, full_hbm, sems.at[sent_hbm.shape[0]]))
    for copy in copies:
        copy.wait()


def carry_kernel(chips, came, full_hbm, feature, rate, out_hbm, full, out, sems):
    lanes = owned_lanes(chips, came.shape[2])
    arriving = started(full_hbm, full, sems.at[0])
    pace = rate[:, lanes]
    taps = taps_of(feature)
    me = lax.axis_index(FAR)
    peers = full.shape[0]
    span = float(ROWS * peers)
    e_group = jnp.exp(-span * pace)
    g_first = jnp.exp(-(span - 1.0) * pace)
    g_second = jnp.exp(-(span - 2.0) * pace)
    e_block = jnp.exp(-float(ROWS) * pace)
    e_first = jnp.exp(-float(ROWS - 1) * pace)
    e_second = jnp.exp(-float(ROWS - 2) * pace)
    carry = jnp.zeros_like(pace)
    before = jnp.zeros((8, pace.shape[1]), F32)
    own0 = jnp.zeros((1, pace.shape[1]), F32)
    own1 = own0
    for i in range(came.shape[0]):
        block = came[i].astype(F32)
        u0, u1 = first_two(taps, block[16:24], before)
        before = block[16:24]
        total = block[0:MODES] + g_first * u0 + g_second * u1
        carry = jnp.where(i < me, e_group * carry + total, carry)
        own0 = jnp.where(i == me, u0, own0)
        own1 = jnp.where(i == me, u1, own1)
    arriving.wait()
    out[0] = carry.astype(BF16)
    carry = e_block * carry + (full[0] + e_first * own0 + e_second * own1)
    for i in range(1, peers):
        out[i] = carry.astype(BF16)
        carry = e_block * carry + full[i]
    started(out, out_hbm, sems.at[1]).wait()


def reach_kernel(rate, weight, out):
    place = (lax.broadcasted_iota(jnp.int32, (HALF, LANES), 0) + 1).astype(F32)

    def block(index):
        lanes = lanes_at(index)
        for m in range(MODES):
            out[m, :, lanes] = weight[m : m + 1, lanes] * jnp.exp(-place * rate[m : m + 1, lanes])

    over(rate.shape[1] // LANES, block)


def fill_lags(reach, rate, lags):
    def block(index):
        lanes = lanes_at(index)
        pace = rate[:, lanes]
        far = jnp.exp(-float(HALF) * pace)
        back = jnp.exp(pace)
        low = jnp.zeros((HALF, LANES), F32)
        high = low
        now = jnp.zeros((1, LANES), F32)
        for m in range(MODES):
            tap = reach[m, :, lanes]
            low = low + tap
            high = high + tap * far[m : m + 1]
            now = now + tap[0:1] * back[m : m + 1]
        lags[0:HALF, lanes] = low
        lags[HALF:STEP, lanes] = high
        lags[STEP - 1 : STEP, lanes] = now

    over(rate.shape[1] // LANES, block)


def add_modes(low, high, reach, rows, slot, lanes):
    for m in range(MODES):
        near = reach[m, :, lanes]
        far = near * rows[slot, GROUPS * MODES + m : GROUPS * MODES + m + 1]
        for g in range(GROUPS):
            state = rows[slot, g * MODES + m : g * MODES + m + 1]
            low[g] = low[g] + near * state
            high[g] = high[g] + far * state


SHORT_PIECES = 4


def short_kernel(
    gate_hbm, key_hbm, value_hbm, rim_hbm, feature_hbm, taps_hbm, out_hbm, gate, key, value, rim, feature, taps, out, kw, vw, gw, uw, sems, outs
):
    width = key.shape[1]

    def large(index):
        span = piece(width, SHORT_PIECES, index)
        return [
            pltpu.make_async_copy(a.at[:, span], b.at[:, span], sems.at[3 + 3 * index + j])
            for j, (a, b) in enumerate(((gate_hbm, gate), (key_hbm, key), (value_hbm, value)))
        ]

    def leaving(index):
        span = piece(width, SHORT_PIECES, index)
        return pltpu.make_async_copy(out.at[:, span], out_hbm.at[:, span], outs.at[index])

    small = [
        started(rim_hbm, rim, sems.at[0]),
        started(feature_hbm, feature, sems.at[1]),
        started(taps_hbm, taps, sems.at[2]),
    ]
    for index in range(SHORT_PIECES):
        for copy in large(index):
            copy.start()
    for slot in range(2):
        kw[slot, 0:8] = jnp.zeros((8, LANES), F32)
        vw[slot, 0:8] = jnp.zeros((8, LANES), F32)
        gw[slot, 0:16] = jnp.zeros((16, LANES), F32)
    for copy in small:
        copy.wait()

    def one(block, slot):
        lanes = lanes_at(block)
        halo = rim[:, lanes].astype(F32)
        kw[slot, 8:16] = halo[0:8]
        kw[slot, 16 : 16 + ROWS] = key[:, lanes].astype(F32)
        vw[slot, 8:16] = halo[8:16]
        vw[slot, 16 : 16 + ROWS] = value[:, lanes].astype(F32)
        gw[slot, 14:16] = halo[16:18]
        gw[slot, 16 : 16 + ROWS] = gate[:, lanes].astype(F32)

        def feat(w, stream, start, count):
            f = [feature[j, stream : stream + 1, lanes] for j in range(3)]
            return (
                f[0] * w[slot, start : start + count]
                + f[1] * w[slot, start - 1 : start - 1 + count]
                + f[2] * w[slot, start - 2 : start - 2 + count]
            )

        u = feat(kw, 1, 8, ROWS + 8) * feat(vw, 2, 8, ROWS + 8)
        uw[slot] = u.astype(BF16).astype(F32)
        mixed = taps[0:1, lanes] * uw[slot, 8 : 8 + ROWS]
        for lag in range(1, taps.shape[0]):
            mixed = mixed + taps[lag : lag + 1, lanes] * uw[slot, 8 - lag : 8 - lag + ROWS]
        out[:, lanes] = (feat(gw, 0, 16, ROWS) * mixed).astype(BF16)

    each = width // SHORT_PIECES // LANES // 2

    def some(index):
        for copy in large(index):
            copy.wait()

        def pair(inner):
            for slot in range(2):
                one((index * each + inner) * 2 + slot, slot)

        over(each, pair)
        leaving(index).start()

    over(SHORT_PIECES, some)
    for index in range(SHORT_PIECES):
        leaving(index).wait()


LOCAL_PIECES = 4


def local_kernel(
    gate_hbm, key_hbm, value_hbm, rim_hbm, feature_hbm, skip_hbm, kept_hbm, reach, rate, out, gate, key, value, rim, feature, skip, lags, kept, kw, vw, gw, uw, rows, sems
):
    width = key.shape[1]

    def large(index):
        span = piece(width, LOCAL_PIECES, index)
        pairs = ((gate_hbm, gate), (key_hbm, key), (value_hbm, value))
        return [
            pltpu.make_async_copy(a.at[:, span], b.at[:, span], sems.at[4 + 4 * index + j]) for j, (a, b) in enumerate(pairs)
        ] + [pltpu.make_async_copy(kept_hbm.at[:, :, span], kept.at[:, :, span], sems.at[7 + 4 * index])]

    small = [
        started(rim_hbm, rim, sems.at[0]),
        started(feature_hbm, feature, sems.at[1]),
        started(skip_hbm, skip, sems.at[2]),
    ]
    for index in range(LOCAL_PIECES):
        for copy in large(index):
            copy.start()
    for w in (kw, vw, gw, uw):
        for slot in range(2):
            w[slot, 0:16] = jnp.zeros((16, LANES), F32)
    place = lax.broadcasted_iota(jnp.int32, (STEP, LANES), 0)
    fill_lags(reach, rate, lags)
    for copy in small:
        copy.wait()

    def one(block, slot):
        lanes = lanes_at(block)
        halo = rim[:, lanes].astype(F32)
        kw[slot, 14:16] = halo[18:20]
        kw[slot, 16 : 16 + ROWS] = key[:, lanes].astype(F32)
        vw[slot, 14:16] = halo[20:22]
        vw[slot, 16 : 16 + ROWS] = value[:, lanes].astype(F32)
        gw[slot, 14:16] = halo[22:24]
        gw[slot, 16 : 16 + ROWS] = gate[:, lanes].astype(F32)

        def feat(w, stream):
            f = [feature[j, stream : stream + 1, lanes] for j in range(3)]
            return f[0] * w[slot, 16 : 16 + ROWS] + f[1] * w[slot, 15 : 15 + ROWS] + f[2] * w[slot, 14 : 14 + ROWS]

        out[ROWS : 2 * ROWS, lanes] = feat(gw, 0)
        uw[slot, 16 : 16 + ROWS] = (feat(kw, 1) * feat(vw, 2)).astype(BF16).astype(F32)
        pace = rate[:, lanes]
        jump = jnp.exp(-float(STEP) * pace)
        state = uw[slot, 16:17] * jnp.exp(-float(STEP - 1) * pace) + uw[slot, 17:18] * jnp.exp(-float(STEP - 2) * pace)
        rows[slot, 0:MODES] = jnp.zeros((MODES, LANES), F32)
        for g in range(1, GROUPS):
            rows[slot, g * MODES : (g + 1) * MODES] = kept[g, :, lanes] + state
            state = state * jump
        rows[slot, GROUPS * MODES : (GROUPS + 1) * MODES] = jnp.exp(-float(HALF) * pace)
        now = lags[STEP - 1 : STEP, lanes] + skip[:, lanes]
        low, high = [], []
        for g in range(GROUPS):
            start = 16 + g * STEP
            low.append(now * uw[slot, start : start + HALF])
            high.append(now * uw[slot, start + HALF : start + STEP])
        for lag in range(1, STEP):
            tap = jnp.where(place >= lag, lags[lag - 1 : lag, lanes], 0.0)
            for g in range(GROUPS):
                start = 16 + g * STEP - lag
                if lag < HALF:
                    low[g] = low[g] + tap[0:HALF] * uw[slot, start : start + HALF]
                high[g] = high[g] + tap[HALF:STEP] * uw[slot, start + HALF : start + STEP]
        add_modes(low, high, reach, rows, slot, lanes)
        for g in range(GROUPS):
            out[g * STEP : g * STEP + HALF, lanes] = low[g]
            out[g * STEP + HALF : (g + 1) * STEP, lanes] = high[g]

    each = width // LOCAL_PIECES // LANES // 2
    for index in range(LOCAL_PIECES):
        for copy in large(index):
            copy.wait()

        def pair(inner):
            for slot in range(2):
                one((index * each + inner) * 2 + slot, slot)

        over(each, pair)


FINISH_PIECES = 4


def finish_kernel(came, local, reach, rate, out_hbm, out, rows, outs):
    width = rate.shape[1]

    def leaving(index):
        span = piece(width, FINISH_PIECES, index)
        return pltpu.make_async_copy(out.at[:, span], out_hbm.at[:, span], outs.at[index])

    each = width // FINISH_PIECES // LANES // 2

    def one(owner, slot):
        lanes = lanes_at(owner * 2 + slot)
        state = came[owner, :, slot * LANES : (slot + 1) * LANES].astype(F32)
        rows[slot, 0:MODES] = state
        rows[slot, MODES : 2 * MODES] = jnp.exp(-float(HALF) * rate[:, lanes])
        totals = [local[k * HALF : (k + 1) * HALF, lanes] for k in range(ROWS // HALF)]
        for m in range(MODES):
            term = reach[m, :, lanes] * rows[slot, m : m + 1]
            hop = jnp.broadcast_to(rows[slot, MODES + m : MODES + m + 1], (HALF, LANES))
            for k in range(ROWS // HALF):
                totals[k] = totals[k] + term
                term = term * hop
        for g in range(GROUPS):
            total = local[ROWS + g * STEP : ROWS + (g + 1) * STEP, lanes] * jnp.concatenate(totals[2 * g : 2 * g + 2], axis=0)
            out[g * STEP : (g + 1) * STEP, lanes] = total.astype(BF16)

    def some(index):
        def pair(inner):
            for slot in range(2):
                one(index * each + inner, slot)

        over(each, pair)
        leaving(index).start()

    over(FINISH_PIECES, some)
    for index in range(FINISH_PIECES):
        leaving(index).wait()


def shards(
    se_gate,
    se_key,
    se_value,
    li_gate,
    li_key,
    li_value,
    se_feature,
    se_filter,
    li_feature,
    li_residue,
    li_rate,
    li_skip,
):
    width = se_gate.shape[1]
    chips = lax.axis_size("chip")
    near = lax.axis_size(NEAR)
    far = lax.axis_size(FAR)
    part = width // near
    swap = lambda value, axis: lax.all_to_all(value, axis, split_axis=0, concat_axis=0, tiled=True)
    dma = pltpu.SemaphoreType.DMA
    stream = room(ROWS, width, dtype=BF16)
    padded = room(2, 16 + ROWS, LANES)
    rim_room = room(32, width, dtype=BF16)
    feature_room = room(*li_feature.shape)

    kept, sent, rim = call(
        states_kernel,
        "states",
        [HBM] * 8,
        [(slow(GROUPS, MODES, width), HBM), (slow(near, 24, part, dtype=BF16), HBM), (fast(32, width, dtype=BF16), AUTO)],
        [
            stream,
            stream,
            feature_room,
            room(MODES, width),
            room(GROUPS, MODES, width),
            room(near, 24, part),
            room(near, 24, part, dtype=BF16),
            room(2, 3, 8 + ROWS, LANES),
            room(CHUNK, ROWS, LANES),
            room(4, 16, width, dtype=BF16),
            room(32, width),
            dma((2 + 2 * (width // (CHUNK * LANES)),)),
            dma((2 * (width // (CHUNK * LANES)),)),
            dma((4,)),
        ],
        12000000,
        3000000,
    )(li_key, li_value, li_feature, li_rate, se_gate, se_key, se_value, li_gate)

    came = swap(sent, NEAR)
    rim = call(rim_kernel, "rim", [AUTO], [(fast(32, width, dtype=BF16), AUTO)], [], 1000000, 500000)(rim)
    weight = li_residue * jnp.sqrt(-jnp.expm1(-2.0 * li_rate))
    reach = call(
        reach_kernel, "reach", [AUTO] * 2, [(fast(MODES, HALF, width), AUTO)], [], 3000000, 2000000
    )(li_rate, weight)
    came, reach = lax.optimization_barrier((came, reach))

    group, full, taps = call(
        functools.partial(group_kernel, chips),
        "group",
        [AUTO] * 3,
        [(slow(far, 24, part, dtype=BF16), HBM), (slow(near, MODES, part), HBM), (fast(3, 3, part), AUTO)],
        [room(24, part, dtype=BF16), room(near, MODES, part), dma((far + 1,))],
        500000,
        500000,
    )(came, li_feature, li_rate)

    groups = swap(group, FAR)
    count = lax.axis_size(PART)
    halo = lax.ppermute(rim, PART, [(i, i + 1) for i in range(count - 1)])
    local = call(
        local_kernel,
        "local",
        [HBM] * 7 + [AUTO] * 2,
        [(fast(2 * ROWS, width), AUTO)],
        [
            stream,
            stream,
            stream,
            rim_room,
            feature_room,
            room(1, width),
            room(STEP, width),
            room(GROUPS, MODES, width),
            padded,
            padded,
            padded,
            padded,
            room(2, (GROUPS + 1) * MODES, LANES),
            dma((4 + 4 * LOCAL_PIECES,)),
        ],
        LOCAL_FLOPS,
        3000000,
    )(li_gate, li_key, li_value, halo, li_feature, li_skip.reshape(1, width), kept, reach, li_rate)

    groups, local = lax.optimization_barrier((groups, local))

    states = call(
        functools.partial(carry_kernel, chips),
        "carry",
        [AUTO, HBM, AUTO, AUTO],
        [(slow(near, MODES, part, dtype=BF16), HBM)],
        [room(near, MODES, part), room(near, MODES, part, dtype=BF16), dma((2,))],
        500000,
        500000,
    )(groups, full, taps, li_rate)

    back = swap(states, NEAR)
    se_out = call(
        short_kernel,
        "short",
        [HBM] * 6,
        [(slow(ROWS, width, dtype=BF16), HBM)],
        [
            stream,
            stream,
            stream,
            rim_room,
            feature_room,
            room(*se_filter.shape),
            stream,
            padded,
            padded,
            padded,
            room(2, 8 + ROWS, LANES),
            dma((3 + 3 * SHORT_PIECES,)),
            dma((SHORT_PIECES,)),
        ],
        12000000,
        2000000,
    )(se_gate, se_key, se_value, halo, se_feature, se_filter)
    li_out = call(
        finish_kernel,
        "finish",
        [AUTO] * 4,
        [(slow(ROWS, width, dtype=BF16), HBM)],
        [stream, room(2, 2 * MODES, LANES), dma((FINISH_PIECES,))],
        10000000,
        5000000,
    )(back, local, reach, li_rate)
    return (se_out, li_out)


def solution(mesh):
    sizes = dict(zip(mesh.axis_names, mesh.devices.shape))
    split = mesh.devices.reshape(sizes["dp"], sizes["node"] // 2, 2, sizes["chip"])
    inner = Mesh(split, ("dp", "far", "core", "chip"))
    rows = P(("dp", "far", "core", "chip"), None)
    return jax.shard_map(
        shards,
        mesh=inner,
        in_specs=(rows,) * 6 + (P(),) * 6,
        out_specs=(rows, rows),
        check_vma=False,
    )
```
